32 devices in a mesh: ctx: 2 (over y), fsdp: 16 (over z, x, core).
Axes of the slice: x: 2, y: 2, z: 4, core: 2. Of those that a mesh axis runs over, the one named last changes fastest.
Arguments:
- hidden_rows: bfloat16 [16, 256, 4608], P('fsdp', 'ctx'), may hold values from -6 to 6
- query_proj: bfloat16 [16, 256, 2048], P('fsdp', 'ctx'), may hold values from -10 to 10
- key_proj: bfloat16 [16, 256, 1024], P('fsdp', 'ctx'), may hold values from -10 to 10
- value_proj: bfloat16 [16, 256, 1024], P('fsdp', 'ctx'), may hold values from -6 to 6
- order_pos: int32 [16, 256], P('fsdp', 'ctx'), may hold values from 0 to 255, each once within a row
- post_gain: float32 [4608], replicated, may hold values from 0.5 to 1.5
- out_weight: bfloat16 [2048, 4608], P('fsdp', 'ctx'), may hold values from -0.125 to 0.125
Outputs:
- residual_out: bfloat16 [16, 256, 4608], P('fsdp', 'ctx')
The draws below stay inside these ranges and needn't reach their ends.
Inputs may be any that keep to these rules, and one draw needn't show every extreme that they name: Each document's row of order_pos holds every position of 0 to 255 exactly once.
All inputs are finite; a program needn't handle non-finite values.
Results may differ from the reference program's by a relative error of at most 0.0053.
Values may be sent and summed in bfloat16 or wider, within the bound.
No kernel may reach another device: no remote copies, remote signals or barrier semaphores. Data moves between devices by JAX's collectives and lax.ppermute only.
A program may use at most 64 MiB of HBM per device.

```python
import jax
import jax.numpy as jnp
from jax import lax

D = 4608
HQ = 16
HK = 8
DH = 128
LENGTH = 256
DOCS = 16


def steps_of(stream_key, shape, pieces, smallest, largest):
    loudness, own = 1.0, jax.random.fold_in(stream_key, 6)
    for axis_at, shards_of in pieces:
        heights = jnp.exp(jax.random.uniform(jax.random.fold_in(own, axis_at), (shards_of,), jnp.float32, smallest / len(pieces), largest / len(pieces)))
        loudness = loudness * jnp.repeat(heights, shape[axis_at] // shards_of).reshape([-1 if axis == axis_at else 1 for axis in range(len(shape))])
    return loudness


def centred(stream_key, dims, scale, most, split=(), dtype=jnp.bfloat16):
    array = scale * jax.random.normal(stream_key, dims, jnp.float32)
    if split:
        array = array * steps_of(stream_key, dims, split, -0.22, 0.18)
    return jnp.clip(array, -most, most).astype(dtype)


def setup_inputs(seed: int = 0) -> dict:
    streams_of = jax.random.split(jax.random.key(seed), 8)
    return {
        "hidden_rows": centred(streams_of[0], (DOCS, LENGTH, D), 1.0, 6.0, ((0, 16), (1, 2))),
        "query_proj": centred(streams_of[1], (DOCS, LENGTH, HQ * DH), 1.7, 10.0, ((0, 16), (1, 2))),
        "key_proj": centred(streams_of[2], (DOCS, LENGTH, HK * DH), 1.7, 10.0, ((0, 16), (1, 2))),
        "value_proj": centred(streams_of[3], (DOCS, LENGTH, HK * DH), 1.0, 6.0, ((0, 16), (1, 2))),
        "order_pos": jax.vmap(lambda own: jax.random.permutation(own, LENGTH))(jax.random.split(streams_of[4], DOCS)).reshape((DOCS, LENGTH)).astype(jnp.int32),
        "post_gain": jnp.clip(1.0 + 0.1 * jax.random.normal(streams_of[5], (D,), jnp.float32), 0.5, 1.5),
        "out_weight": centred(streams_of[6], (HQ * DH, D), (HQ * DH) ** -0.5, 0.125, ((0, 16), (1, 2))),
    }


score_scale = 1.0 / 12.0
soft_cap = 50.0
norm_eps = 1e-06

def reference(hidden_rows, query_proj, key_proj, value_proj, order_pos, post_gain, out_weight):
    groups = HQ // HK

    def score_document(operands):
        hidden_doc, query_rows, key_rows, value_rows, position = operands
        query_heads = query_rows.astype(jnp.float32).reshape(LENGTH, HK, groups, DH)
        key_heads = key_rows.astype(jnp.float32).reshape(LENGTH, HK, DH)
        value_heads = value_rows.astype(jnp.float32).reshape(LENGTH, HK, DH)
        scores = jnp.einsum('thgd,nhd->hgtn', query_heads, key_heads) * score_scale
        capped = soft_cap * jnp.tanh(scores / soft_cap)
        visible = position[None, :] <= position[:, None]
        weights = jnp.where(visible, jnp.exp(capped), jnp.float32(0.0))
        rounded = lax.optimization_barrier(weights.astype(jnp.bfloat16)).astype(jnp.float32)
        numerator = jnp.einsum('hgtn,nhd->thgd', rounded, value_heads)
        denominator = jnp.transpose(lax.optimization_barrier(jnp.sum(weights, axis=-1)), (2, 0, 1))
        attended = (numerator / denominator[..., None]).astype(jnp.bfloat16).reshape(LENGTH, HQ * DH)
        projected = jnp.dot(attended, out_weight, preferred_element_type=jnp.float32).astype(jnp.bfloat16)
        widened = projected.astype(jnp.float32)
        normed = widened * lax.rsqrt(lax.optimization_barrier(jnp.mean(widened * widened, axis=-1, keepdims=True)) + norm_eps) * post_gain
        return (hidden_doc.astype(jnp.float32) + normed).astype(jnp.bfloat16)
    return lax.map(score_document, (hidden_rows, query_proj, key_proj, value_proj, order_pos))
```

```python
import functools

import jax
import jax.numpy as jnp
import numpy as np
from jax import lax
from jax.experimental import pallas as pl
from jax.experimental.pallas import tpu as pltpu
from jax.sharding import Mesh
from jax.sharding import PartitionSpec as P

HQ = 16
HK = 8
DH = 128

score_scale = 1.0 / 12.0
soft_cap = 50.0
norm_eps = 1e-06

CHUNKS = (640, 512)
VMEM_LIMIT = 56 * 2**20
VMEM = pl.BlockSpec(memory_space=pltpu.VMEM)
ANY = pl.BlockSpec(memory_space=pl.ANY)


def params():
    return pltpu.CompilerParams(vmem_limit_bytes=VMEM_LIMIT)


def bf16(*dims):
    return jax.ShapeDtypeStruct(dims, jnp.bfloat16)


def ring_of(n):
    return list(range(0, 2, 1))[:1] + list(range(1, n, 2)) + list(range(2, n, 2))[::-1]


def cut_weight(w_ref, *rest):
    outs, sems = rest[:-1], rest[-1]
    quarter = w_ref.shape[1] // 2
    me = lax.axis_index("x")
    copies = []
    start = 0
    for i, (out, side) in enumerate(zip(outs, (me, 1 - me, 1 - me))):
        if i == 2:
            start = outs[1].shape[1]
        at = pl.multiple_of(side * quarter + start, 128)
        copies.append(
            pltpu.make_async_copy(w_ref.at[:, pl.ds(at, out.shape[1])], out, sems.at[i])
        )
    for copy in copies:
        copy.start()
    for copy in copies:
        copy.wait()


def attend(q_ref, k_own, k_far, v_own, v_far, pos_own, pos_far, *outs):
    tokens = q_ref.shape[0]
    groups = HQ // HK
    own = pos_own[...].astype(jnp.float32)
    far = pos_far[...].astype(jnp.float32)
    mine = jnp.transpose(jnp.broadcast_to(own, (tokens, tokens)))[:, :1]
    visible = jnp.concatenate([own, far], axis=1) <= mine
    visible = jnp.concatenate([visible] * groups, axis=0)
    for head in range(HK):
        at = pl.ds(head * DH, DH)
        query = jnp.concatenate(
            [q_ref[:, pl.ds((head * groups + g) * DH, DH)] for g in range(groups)], axis=0
        )
        keys = jnp.concatenate([k_own[:, at], k_far[:, at]], axis=0)
        values = jnp.concatenate([v_own[:, at], v_far[:, at]], axis=0)
        scores = lax.dot_general(
            query, keys, (((1,), (1,)), ((), ())), preferred_element_type=jnp.float32
        )
        capped = soft_cap * jnp.tanh(scores * (score_scale / soft_cap))
        weights = jnp.where(visible, jnp.exp(capped), 0.0)
        total = jnp.sum(weights, axis=-1, keepdims=True)
        mixed = jnp.dot(weights.astype(jnp.bfloat16), values, preferred_element_type=jnp.float32)
        mixed = (mixed / total).astype(jnp.bfloat16)
        for g in range(groups):
            h = head * groups + g
            per = HQ // len(outs)
            outs[h // per][:, pl.ds((h % per) * DH, DH)] = mixed[g * tokens : (g + 1) * tokens]


def head_of(step, same_x, same_core, ring):
    z, x, core = (lax.axis_index(name) for name in ("z", "x", "core"))
    n = len(ring)
    source = 0
    for i, stop in enumerate(ring):
        source = source + jnp.where(z == stop, ring[(i - step) % n], 0)
    x = x if same_x else 1 - x
    core = core if same_core else 1 - core
    return (source * 2 + x) * 2 + core


def project(ring, first, groups, halves, *refs):
    n = len(ring)
    acts = refs[: groups * halves]
    near = refs[groups * halves : groups * halves + 2 * n]
    away = refs[groups * halves + 2 * n : groups * halves + 4 * n]
    outs = refs[groups * halves + 4 * n : groups * halves + 4 * n + groups]
    a_all, w_all = refs[-2:]
    tokens, columns = outs[0].shape
    wide = acts[0].shape[1]
    for g in range(groups):
        for half in range(halves):
            a_all[pl.ds(g * tokens, tokens), pl.ds(half * wide, wide)] = acts[g * halves + half][...]
    for same_x, bufs, at in ((True, near, first), (False, away, 0)):
        for step in range(n):
            for other, same_core in enumerate((True, False)):
                head = head_of(step, same_x, same_core, ring)
                w_all[pl.ds(pl.multiple_of(head * DH, DH), DH), :] = bufs[step * 2 + other][
                    :, pl.ds(at, columns)
                ]
    for g in range(groups // 2):
        rows = jnp.dot(
            a_all[pl.ds(g * 2 * tokens, 2 * tokens), :], w_all[...], preferred_element_type=jnp.float32
        ).astype(jnp.bfloat16)
        outs[2 * g][...] = rows[:tokens]
        outs[2 * g + 1][...] = rows[tokens:]


def finish(chunks, hidden_ref, gain_ref, *refs):
    pieces, out_ref = refs[:-1], refs[-1]
    width = hidden_ref.shape[1]
    x, y = lax.axis_index("x"), lax.axis_index("ctx")
    owners = ((x, y), (1 - x, y), (x, 1 - y), (1 - x, 1 - y))
    total = 0.0
    for piece in pieces:
        value = piece[...].astype(jnp.float32)
        total = total + jnp.sum(value * value, axis=-1, keepdims=True)
    scale = lax.rsqrt(total / width + norm_eps)
    start = 0
    for c, columns in enumerate(chunks):
        for i, (px, py) in enumerate(owners):
            at = pl.ds(pl.multiple_of((py * 2 + px) * (width // 4) + start, 128), columns)
            normed = pieces[c * 4 + i][...].astype(jnp.float32) * scale * gain_ref[:, at]
            out_ref[:, at] = (hidden_ref[:, at].astype(jnp.float32) + normed).astype(jnp.bfloat16)
        start += columns


def shards(ring, chunks, hidden_rows, query_proj, key_proj, value_proj, order_pos, post_gain, out_weight):
    n = len(ring)
    tokens = query_proj.shape[1]
    width = hidden_rows.shape[2]
    swap = [(0, 1), (1, 0)]
    along = [(ring[i], ring[(i + 1) % n]) for i in range(n)]

    def over(value, axis):
        if axis == "diag":
            return lax.ppermute(value, ("ctx", "x"), [(i, 3 - i) for i in range(4)])
        return lax.ppermute(value, axis, along if axis == "z" else swap)

    query, key, value = query_proj[0], key_proj[0], value_proj[0]
    pos_far = over(order_pos, "ctx")
    key_far = over(key, "ctx")
    value_far = over(value, "ctx")

    quarter = out_weight.shape[1] // 2
    rows = out_weight.shape[0]
    near, *sent = pl.pallas_call(
        cut_weight,
        out_shape=[bf16(rows, quarter)] + [bf16(rows, c) for c in chunks],
        in_specs=[ANY],
        out_specs=[VMEM] * 3,
        scratch_shapes=[pltpu.SemaphoreType.DMA((3,))],
        compiler_params=params(),
        name="cut_weight",
    )(out_weight)
    away = [over(piece, "x") for piece in sent]

    def gather(piece):
        held = [piece]
        for _ in range(n - 1):
            held.append(over(held[-1], "z"))
        both = []
        for piece in held:
            both += [piece, over(piece, "core")]
        return both

    near = gather(near)
    away = [gather(piece) for piece in away]

    halves = 2
    acts = pl.pallas_call(
        attend,
        out_shape=[bf16(tokens, HQ * DH // halves)] * halves,
        in_specs=[VMEM] * 7,
        out_specs=[VMEM] * halves,
        compiler_params=params(),
        cost_estimate=pl.CostEstimate(flops=2**28, bytes_accessed=2**21, transcendentals=2**20),
        name="attend",
    )(query, key, key_far, value, value_far, order_pos, pos_far)
    acts_x = [over(a, "x") for a in acts]
    acts_y = [over(a, "ctx") for a in acts]
    acts_d = [over(acts_y[0], "x"), over(acts_x[1], "ctx")]
    all_acts = [*acts, *acts_x, *acts_y, *acts_d]

    pieces = []
    start = 0
    for columns, far in zip(chunks, away):
        out = pl.pallas_call(
            functools.partial(project, ring, start, 4, halves),
            out_shape=[bf16(tokens, columns)] * 4,
            in_specs=[VMEM] * (4 * halves + 4 * n),
            out_specs=[VMEM] * 4,
            scratch_shapes=[
                pltpu.VMEM((4 * tokens, HQ * DH), jnp.bfloat16),
                pltpu.VMEM((HQ * DH, columns), jnp.bfloat16),
            ],
            compiler_params=params(),
            cost_estimate=pl.CostEstimate(
                flops=8 * tokens * HQ * DH * columns, bytes_accessed=2**22, transcendentals=0
            ),
            name="project",
        )(*all_acts, *near, *far)
        pieces += [out[0], over(out[1], "x"), over(out[2], "ctx"), over(out[3], "diag")]
        start += columns

    out = pl.pallas_call(
        functools.partial(finish, chunks),
        out_shape=bf16(tokens, width),
        in_specs=[VMEM] * (2 + len(pieces)),
        out_specs=VMEM,
        compiler_params=params(),
        name="finish",
    )(hidden_rows[0], post_gain.reshape(1, width), *pieces)
    return out[None]


def plain_shards(hidden_rows, query_proj, key_proj, value_proj, order_pos, post_gain, out_weight):
    tokens = query_proj.shape[1]
    groups = HQ // HK
    positions = lax.all_gather(order_pos, "ctx", axis=1, tiled=True)[0]
    weight_block = lax.all_gather(out_weight, "fsdp", axis=0, tiled=True)
    query = query_proj[0].reshape(tokens, HK, groups, DH)
    keys = lax.all_gather(key_proj, "ctx", axis=1, tiled=True)[0].reshape(-1, HK, DH)
    values = lax.all_gather(value_proj, "ctx", axis=1, tiled=True)[0].reshape(-1, HK, DH)
    scores = jnp.einsum("thgd,nhd->hgtn", query, keys, preferred_element_type=jnp.float32)
    capped = soft_cap * jnp.tanh(scores * score_scale / soft_cap)
    visible = positions[None, :] <= order_pos[0][:, None]
    weights = jnp.where(visible, jnp.exp(capped), 0.0)
    numerator = jnp.einsum(
        "hgtn,nhd->thgd", weights.astype(jnp.bfloat16), values, preferred_element_type=jnp.float32
    )
    denominator = jnp.transpose(jnp.sum(weights, axis=-1), (2, 0, 1))
    attended = (numerator / denominator[..., None]).astype(jnp.bfloat16).reshape(1, tokens, HQ * DH)
    projected = jnp.dot(
        lax.all_gather(attended, "ctx", axis=1, tiled=True)[0],
        weight_block,
        preferred_element_type=jnp.float32,
    )
    token_rows = lax.all_to_all(
        projected.astype(jnp.bfloat16), "ctx", split_axis=0, concat_axis=1, tiled=True
    ).astype(jnp.float32)
    mean = jnp.mean(token_rows * token_rows, axis=-1, keepdims=True)
    normed = token_rows * lax.rsqrt(mean + norm_eps) * post_gain
    return (hidden_rows[0].astype(jnp.float32) + normed).astype(jnp.bfloat16)[None]


def solution(mesh):
    ctx, fsdp = mesh.shape["ctx"], mesh.shape["fsdp"]
    rows = "fsdp"
    body = plain_shards
    if ctx == 2 and fsdp % 4 == 0 and fsdp == HQ:
        mesh = Mesh(np.asarray(mesh.devices).reshape(ctx, fsdp // 4, 2, 2), ("ctx", "z", "x", "core"))
        rows = ("z", "x", "core")
        body = functools.partial(shards, ring_of(fsdp // 4), CHUNKS)
    placed = (
        P(rows, "ctx", None),
        P(rows, "ctx", None),
        P(rows, "ctx", None),
        P(rows, "ctx", None),
        P(rows, "ctx"),
        P(),
        P(rows, "ctx"),
    )
    return jax.shard_map(
        body, mesh=mesh, in_specs=placed, out_specs=P(rows, "ctx", None), check_vma=False
    )
```

```python
import functools

import jax
import jax.numpy as jnp
import numpy as np
from jax import lax
from jax.experimental import pallas as pl
from jax.experimental.pallas import tpu as pltpu
from jax.sharding import Mesh
from jax.sharding import PartitionSpec as P

HQ = 16
HK = 8
DH = 128

score_scale = 1.0 / 12.0
soft_cap = 50.0
norm_eps = 1e-06

CHUNKS = (640, 512)
TIES = {'rd2': ('rd1',), 'd1': ('B1',), 'cB0': ('y2',), 'cB1': ('B2',), 'ca0': ('cB0',)}
COSTS = {'att': 3000, 'cut': 1500, 'stage': 9000, 'finish': 1500, 'proj1': 6000}
PER_CYCLE = 524288
FIRST = ()
ACTS = 2
WHOLE = 2
VMEM_LIMIT = 14 * 2**20
VMEM = pl.BlockSpec(memory_space=pltpu.VMEM)
HBM = pl.BlockSpec(memory_space=pl.ANY)


def params():
    return pltpu.CompilerParams(vmem_limit_bytes=VMEM_LIMIT)


def bf16(*dims):
    return jax.ShapeDtypeStruct(dims, jnp.bfloat16)


def ring_of(n):
    return list(range(0, 2, 1))[:1] + list(range(1, n, 2)) + list(range(2, n, 2))[::-1]


def cut(w_ref, near, away):
    quarter = near.shape[1]
    me = lax.axis_index("x")
    near[...] = w_ref[:, pl.ds(pl.multiple_of(me * quarter, 128), quarter)]
    away[...] = w_ref[:, pl.ds(pl.multiple_of((1 - me) * quarter, 128), quarter)]


def stage(*refs):
    half = len(refs) // 2
    for ref, out in zip(refs[:half], refs[half:]):
        out[...] = ref[...]


def split(ref, *outs):
    start = 0
    for out in outs:
        out[...] = ref[:, pl.ds(start, out.shape[1])]
        start += out.shape[1]


def attend(q_ref, k_own, k_far, v_own, v_far, pos_own, pos_far, *outs):
    tokens = q_ref.shape[0]
    groups = HQ // HK
    per = HQ // len(outs)
    own = pos_own[...].astype(jnp.float32)
    far = pos_far[...].astype(jnp.float32)
    mine = jnp.transpose(jnp.broadcast_to(own, (tokens, tokens)))[:, :1]
    visible = jnp.concatenate([own, far], axis=1) <= mine
    visible = jnp.concatenate([visible] * groups, axis=0)
    for head in range(HK):
        at = pl.ds(head * DH, DH)
        q_at = [pl.ds((head * groups + g) * DH, DH) for g in range(groups)]
        query = jnp.concatenate([q_ref[:, each] for each in q_at], axis=0)
        keys = jnp.concatenate([k_own[:, at], k_far[:, at]], axis=0)
        values = jnp.concatenate([v_own[:, at], v_far[:, at]], axis=0)
        scores = lax.dot_general(
            query, keys, (((1,), (1,)), ((), ())), preferred_element_type=jnp.float32
        )
        capped = soft_cap * jnp.tanh(scores * (score_scale / soft_cap))
        weights = jnp.where(visible, jnp.exp(capped), 0.0)
        total = jnp.sum(weights, axis=-1, keepdims=True)
        mixed = jnp.dot(weights.astype(jnp.bfloat16), values, preferred_element_type=jnp.float32)
        mixed = (mixed / total).astype(jnp.bfloat16)
        for g in range(groups):
            h = head * groups + g
            outs[h // per][:, pl.ds((h % per) * DH, DH)] = mixed[g * tokens : (g + 1) * tokens]


def head_of(step, same_x, same_core, ring):
    z, x, core = (lax.axis_index(name) for name in ("z", "x", "core"))
    n = len(ring)
    source = 0
    for i, stop in enumerate(ring):
        source = source + jnp.where(z == stop, ring[(i - step) % n], 0)
    x = x if same_x else 1 - x
    core = core if same_core else 1 - core
    return (source * 2 + x) * 2 + core


def project(ring, first, sizes, *refs):
    n = len(ring)
    count = sum(sizes)
    acts, bufs, outs = refs[:count], refs[count : count + 4 * n], refs[count + 4 * n : -2]
    a_all, w_all = refs[-2:]
    tokens, columns = outs[0].shape
    taken = 0
    for g, parts in enumerate(sizes):
        at = 0
        for act in acts[taken : taken + parts]:
            a_all[pl.ds(g * tokens, tokens), pl.ds(at, act.shape[1])] = act[...]
            at += act.shape[1]
        taken += parts
    for i, buf in enumerate(bufs):
        same_x, step, same_core = i < 2 * n, i // 2 % n, i % 2 == 0
        head = head_of(step, same_x, same_core, ring)
        at = 0 if buf.shape[1] == columns else first
        w_all[pl.ds(pl.multiple_of(head * DH, DH), DH), :] = buf[:, pl.ds(at, columns)]
    for g in range(0, len(outs), 2):
        rows = jnp.dot(
            a_all[pl.ds(g * tokens, 2 * tokens), :], w_all[...], preferred_element_type=jnp.float32
        ).astype(jnp.bfloat16)
        outs[g][...] = rows[:tokens]
        outs[g + 1][...] = rows[tokens:]


def finish(chunks, hidden_ref, gain_ref, *refs):
    pieces, out_ref = refs[:-1], refs[-1]
    width = hidden_ref.shape[1]
    x, y = lax.axis_index("x"), lax.axis_index("ctx")
    owners = ((x, y), (1 - x, y), (x, 1 - y), (1 - x, 1 - y))
    total = 0.0
    for piece in pieces:
        value = piece[...].astype(jnp.float32)
        total = total + jnp.sum(value * value, axis=-1, keepdims=True)
    scale = lax.rsqrt(total / width + norm_eps)
    start = 0
    for c, columns in enumerate(chunks):
        for i, (px, py) in enumerate(owners):
            at = pl.ds(pl.multiple_of((py * 2 + px) * (width // 4) + start, 128), columns)
            normed = pieces[c * 4 + i][...].astype(jnp.float32) * scale * gain_ref[:, at]
            out_ref[:, at] = (hidden_ref[:, at].astype(jnp.float32) + normed).astype(jnp.bfloat16)
        start += columns


def shards(ring, chunks, hidden_rows, query_proj, key_proj, value_proj, order_pos, post_gain, out_weight):
    n = len(ring)
    tokens = query_proj.shape[1]
    width = hidden_rows.shape[2]
    swap = [(0, 1), (1, 0)]
    along = [(ring[i], ring[(i + 1) % n]) for i in range(n)]

    def over(value, axis):
        if axis == "diag":
            return lax.ppermute(value, ("ctx", "x"), [(i, 3 - i) for i in range(4)])
        return lax.ppermute(value, axis, along if axis == "z" else swap)

    rows, block = out_weight.shape
    quarter = block // 2

    def call(body, outs, ins, name, scratch=(), label=None):
        return pl.pallas_call(
            body,
            out_shape=outs,
            in_specs=[VMEM] * ins,
            out_specs=[VMEM] * len(outs),
            scratch_shapes=scratch,
            compiler_params=params(),
            cost_estimate=pl.CostEstimate(
                flops=int(COSTS.get(label or name, 0) * PER_CYCLE) + 1, bytes_accessed=0, transcendentals=0
            ),
            name=name,
        )

    def project_chunk(c, sizes, count):
        columns = chunks[c]
        return call(
            functools.partial(project, ring, sum(chunks[:c]), sizes),
            [bf16(tokens, columns)] * 4,
            count,
            "project",
            [
                pltpu.VMEM((4 * tokens, HQ * DH), jnp.bfloat16),
                pltpu.VMEM((HQ * DH, columns), jnp.bfloat16),
            ],
            label="proj" + str(c + 1),
        )

    moves, kernels = {}, {}
    kernels["cut"] = (call(cut, [bf16(rows, quarter)] * 2, 1, "cut"), ("w",), ("a0", "awayo"))
    kernels["stage"] = (
        call(
            stage,
            [bf16(tokens, a.shape[2]) for a in (query_proj, key_proj, value_proj)]
            + [jax.ShapeDtypeStruct(order_pos.shape, jnp.int32)],
            4,
            "stage",
        ),
        ("qo", "Ko", "Vo", "poso"),
        ("q", "Kq", "Vq", "posq"),
    )
    wide = bf16(tokens, HQ * DH // ACTS)
    halves = "12"[:ACTS]
    for k, axis in (("K", "ctx"), ("V", "ctx"), ("pos", "ctx"), ("B0", "x")):
        moves[k] = ({"B0": "awayo"}.get(k, k + "o"), axis)
    kernels["att"] = (
        call(attend, [wide] * ACTS, 7, "attend", label="att"),
        ("q", "Kq", "K", "Vq", "V", "posq", "pos"),
        tuple("h" + i for i in halves),
    )
    for i in halves:
        moves["x" + i] = ("h" + i, "x")
        moves["y" + i] = ("h" + i, "ctx")
    if ACTS == 2:
        moves["d1"], moves["d2"] = ("y1", "x"), ("x2", "ctx")
        acts = ("h1", "h2", "x1", "x2", "y1", "y2", "d1", "d2")
        sizes = (2, 2, 2, 2)
    else:
        half = bf16(tokens, HQ * DH // 2)
        kernels["hy"] = (call(split, [half] * 2, 1, "halves", label="hy"), ("y1",), ("y1l", "y1r"))
        kernels["hx"] = (call(split, [half] * 2, 1, "halves", label="hx"), ("x1",), ("x1l", "x1r"))
        moves["d1"], moves["d2"] = ("y1l", "x"), ("x1r", "ctx")
        acts, sizes = ("h1", "x1", "y1", "d1", "d2"), (1, 1, 1, 2)
    for i in range(1, n):
        moves["a%d" % i] = ("a%d" % (i - 1), "z")
    for i in range(1, WHOLE + 1):
        moves["B%d" % i] = ("B%d" % (i - 1), "z")
    last = "B%d" % WHOLE
    kernels["split"] = (
        call(split, [bf16(rows, c) for c in chunks], 1, "split"),
        (last,),
        tuple("b%d%d" % (c + 1, WHOLE) for c in range(len(chunks))),
    )
    for c in range(len(chunks)):
        j = str(c + 1)
        for i in range(WHOLE + 1, n):
            moves["b%s%d" % (j, i)] = ("b%s%d" % (j, i - 1), "z")
        away = ["B%d" % i for i in range(WHOLE + 1)] + ["b%s%d" % (j, i) for i in range(WHOLE + 1, n)]
        bufs = []
        for name in ["a%d" % i for i in range(n)] + away:
            moves["c" + name] = (name, "core")
            bufs += [name, "c" + name]
        operands = (*acts, *bufs)
        results = tuple("p" + k + j for k in "oxyd")
        kernels["proj" + j] = (project_chunk(c, sizes, len(operands)), operands, results)
        for k, axis in zip("xyd", ("x", "ctx", "diag")):
            moves["r" + k + j] = ("p" + k + j, axis)

    held = dict(
        w=out_weight, qo=query_proj[0], Ko=key_proj[0], Vo=value_proj[0], poso=order_pos
    )

    def after(value, deps):
        for dep in deps:
            token, held[dep] = lax.optimization_barrier((lax.create_token(), held[dep]))
            token, value = lax.optimization_barrier((token, value))
        return value

    pending = list(kernels) + list(moves)
    pending.sort(key=lambda name: FIRST.index(name) if name in FIRST else len(FIRST))
    while pending:
        for name in pending:
            sources, results = (moves[name][:1], (name,)) if name in moves else kernels[name][1:]
            deps = [d for d in TIES.get(name, ())]
            if all(k in held for k in (*sources, *deps)):
                break
        pending.remove(name)
        first = after(held[sources[0]], deps)
        if name in moves:
            held[name] = over(first, moves[name][1])
        else:
            out = kernels[name][0](first, *(held[k] for k in sources[1:]))
            held.update(zip(results, out))

    pieces = [held[("po" if k == "o" else "r" + k) + str(c + 1)] for c in range(len(chunks)) for k in "oxyd"]

    out = pl.pallas_call(
        functools.partial(finish, chunks),
        out_shape=bf16(tokens, width),
        in_specs=[VMEM] * (2 + len(pieces)),
        out_specs=VMEM,
        compiler_params=params(),
        cost_estimate=pl.CostEstimate(flops=1, bytes_accessed=0, transcendentals=0),
        name="finish",
    )(hidden_rows[0], post_gain.reshape(1, width), *pieces)
    return out[None]


def plain_shards(hidden_rows, query_proj, key_proj, value_proj, order_pos, post_gain, out_weight):
    tokens = query_proj.shape[1]
    groups = HQ // HK
    positions = lax.all_gather(order_pos, "ctx", axis=1, tiled=True)[0]
    weight_block = lax.all_gather(out_weight, "fsdp", axis=0, tiled=True)
    query = query_proj[0].reshape(tokens, HK, groups, DH)
    keys = lax.all_gather(key_proj, "ctx", axis=1, tiled=True)[0].reshape(-1, HK, DH)
    values = lax.all_gather(value_proj, "ctx", axis=1, tiled=True)[0].reshape(-1, HK, DH)
    scores = jnp.einsum("thgd,nhd->hgtn", query, keys, preferred_element_type=jnp.float32)
    capped = soft_cap * jnp.tanh(scores * score_scale / soft_cap)
    visible = positions[None, :] <= order_pos[0][:, None]
    weights = jnp.where(visible, jnp.exp(capped), 0.0)
    numerator = jnp.einsum(
        "hgtn,nhd->thgd", weights.astype(jnp.bfloat16), values, preferred_element_type=jnp.float32
    )
    denominator = jnp.transpose(jnp.sum(weights, axis=-1), (2, 0, 1))
    attended = (numerator / denominator[..., None]).astype(jnp.bfloat16).reshape(1, tokens, HQ * DH)
    projected = jnp.dot(
        lax.all_gather(attended, "ctx", axis=1, tiled=True)[0],
        weight_block,
        preferred_element_type=jnp.float32,
    )
    token_rows = lax.all_to_all(
        projected.astype(jnp.bfloat16), "ctx", split_axis=0, concat_axis=1, tiled=True
    ).astype(jnp.float32)
    mean = jnp.mean(token_rows * token_rows, axis=-1, keepdims=True)
    normed = token_rows * lax.rsqrt(mean + norm_eps) * post_gain
    return (hidden_rows[0].astype(jnp.float32) + normed).astype(jnp.bfloat16)[None]


def solution(mesh):
    ctx, fsdp = mesh.shape["ctx"], mesh.shape["fsdp"]
    rows = "fsdp"
    body = plain_shards
    if ctx == 2 and fsdp % 4 == 0 and fsdp == HQ:
        mesh = Mesh(np.asarray(mesh.devices).reshape(ctx, fsdp // 4, 2, 2), ("ctx", "z", "x", "core"))
        rows = ("z", "x", "core")
        body = functools.partial(shards, ring_of(fsdp // 4), CHUNKS)
    placed = (
        P(rows, "ctx", None),
        P(rows, "ctx", None),
        P(rows, "ctx", None),
        P(rows, "ctx", None),
        P(rows, "ctx"),
        P(),
        P(rows, "ctx"),
    )
    return jax.shard_map(
        body, mesh=mesh, in_specs=placed, out_specs=P(rows, "ctx", None), check_vma=False
    )
```

```python
import functools

import jax
import jax.numpy as jnp
import numpy as np
from jax import lax
from jax.experimental import pallas as pl
from jax.experimental.pallas import tpu as pltpu
from jax.sharding import Mesh
from jax.sharding import PartitionSpec as P

HQ = 16
HK = 8
DH = 128

score_scale = 1.0 / 12.0
soft_cap = 50.0
norm_eps = 1e-06

CHUNKS = (640, 512)
PACKS = (('a0', 'B0', 'a1', 'B1'), ('a2', 'B2'))
WHOLE_STEPS = {'a': 3, 'B': 2}
TIES = {'rx1': ('rd0',), 'B3_0': ('ck0',), 'a2': ('h1',), 'ry1': ('rd0',), 'd1': ('k1',)}
COSTS = {'splitB': 9000, 'hy': 1500, 'proj0': 9000, 'pk0': 1500, 'cut': 9000, 'early': 9000, 'att': 3000, 'stage': 1500, 'pk1': 9000, 'hx': 6000}
PER_CYCLE = 524288
FIRST = ()
ACTS = 1
VMEM_LIMIT = 20 * 2**20
VMEM = pl.BlockSpec(memory_space=pltpu.VMEM)
HBM = pl.BlockSpec(memory_space=pl.ANY)


def params():
    return pltpu.CompilerParams(vmem_limit_bytes=VMEM_LIMIT)


def bf16(*dims):
    return jax.ShapeDtypeStruct(dims, jnp.bfloat16)


def ring_of(n):
    return list(range(0, 2, 1))[:1] + list(range(1, n, 2)) + list(range(2, n, 2))[::-1]


def cut(w_ref, near, away):
    quarter = near.shape[1]
    me = lax.axis_index("x")
    near[...] = w_ref[:, pl.ds(pl.multiple_of(me * quarter, 128), quarter)]
    away[...] = w_ref[:, pl.ds(pl.multiple_of((1 - me) * quarter, 128), quarter)]


def stage(*refs):
    half = len(refs) // 2
    for ref, out in zip(refs[:half], refs[half:]):
        out[...] = ref[...]


def split(ref, *outs):
    start = 0
    for out in outs:
        out[...] = ref[:, pl.ds(start, out.shape[1])]
        start += out.shape[1]


def attend(q_ref, k_own, k_far, v_own, v_far, pos_own, pos_far, *outs):
    tokens = q_ref.shape[0]
    groups = HQ // HK
    per = HQ // len(outs)
    own = pos_own[...].astype(jnp.float32)
    far = pos_far[...].astype(jnp.float32)
    mine = jnp.transpose(jnp.broadcast_to(own, (tokens, tokens)))[:, :1]
    visible = jnp.concatenate([own, far], axis=1) <= mine
    visible = jnp.concatenate([visible] * groups, axis=0)
    for head in range(HK):
        at = pl.ds(head * DH, DH)
        q_at = [pl.ds((head * groups + g) * DH, DH) for g in range(groups)]
        query = jnp.concatenate([q_ref[:, each] for each in q_at], axis=0)
        keys = jnp.concatenate([k_own[:, at], k_far[:, at]], axis=0)
        values = jnp.concatenate([v_own[:, at], v_far[:, at]], axis=0)
        scores = lax.dot_general(
            query, keys, (((1,), (1,)), ((), ())), preferred_element_type=jnp.float32
        )
        capped = soft_cap * jnp.tanh(scores * (score_scale / soft_cap))
        weights = jnp.where(visible, jnp.exp(capped), 0.0)
        total = jnp.sum(weights, axis=-1, keepdims=True)
        mixed = jnp.dot(weights.astype(jnp.bfloat16), values, preferred_element_type=jnp.float32)
        mixed = (mixed / total).astype(jnp.bfloat16)
        for g in range(groups):
            h = head * groups + g
            outs[h // per][:, pl.ds((h % per) * DH, DH)] = mixed[g * tokens : (g + 1) * tokens]


def head_of(step, same_x, same_core, ring):
    z, x, core = (lax.axis_index(name) for name in ("z", "x", "core"))
    n = len(ring)
    source = 0
    for i, stop in enumerate(ring):
        source = source + jnp.where(z == stop, ring[(i - step) % n], 0)
    x = x if same_x else 1 - x
    core = core if same_core else 1 - core
    return (source * 2 + x) * 2 + core


def part(which, ref, out):
    out[...] = ref[:, pl.ds(which * out.shape[1], out.shape[1])]


def stack(*refs):
    bufs, out = refs[:-1], refs[-1]
    for i, buf in enumerate(bufs):
        out[pl.ds(i * buf.shape[0], buf.shape[0]), :] = buf[...]


def stack_acts(sizes, acts, a_all):
    tokens = a_all.shape[0] // len(sizes)
    taken = 0
    for g, parts in enumerate(sizes):
        at = 0
        for act in acts[taken : taken + parts]:
            a_all[pl.ds(g * tokens, tokens), pl.ds(at, act.shape[1])] = act[...]
            at += act.shape[1]
        taken += parts


def columns_of(a_all, heads):
    return jnp.concatenate(
        [a_all[:, pl.ds(pl.multiple_of(head * DH, DH), DH)] for head in heads], axis=1
    )


def early(ring, sizes, heads, *refs):
    count = sum(sizes)
    acts, bufs, (acc, a_all, w_all) = refs[:count], refs[count:-3], refs[-3:]
    stack_acts(sizes, acts, a_all)
    at = 0
    for buf in bufs:
        w_all[pl.ds(at, buf.shape[0]), :] = buf[...]
        at += buf.shape[0]
    heads = [head_of(*head, ring) for head in heads]
    acc[...] = jnp.dot(columns_of(a_all, heads), w_all[...], preferred_element_type=jnp.float32)


def project(ring, first, sizes, heads, acc, a_all, w_all, *refs):
    count = sum(sizes)
    acts, bufs, outs, a_last = refs[:count], refs[count:-5], refs[-5:-1], refs[-1]
    tokens, columns = outs[0].shape
    done = w_all.shape[0] // DH
    stack_acts(sizes, acts, a_last)
    heads = [head_of(*head, ring) for head in heads]
    w_late = jnp.concatenate(
        [buf[:, pl.ds(0 if buf.shape[1] == columns else first, columns)] for buf in bufs], axis=0
    )
    rows = acc[:, pl.ds(first, columns)] + jnp.dot(
        columns_of(a_all, heads[done:]), w_late, preferred_element_type=jnp.float32
    )
    for g in range(3):
        outs[g][...] = rows[g * tokens : (g + 1) * tokens].astype(jnp.bfloat16)
    rows = jnp.dot(
        columns_of(a_last, heads[:done]),
        w_all[:, pl.ds(first, columns)],
        preferred_element_type=jnp.float32,
    ) + jnp.dot(columns_of(a_last, heads[done:]), w_late, preferred_element_type=jnp.float32)
    outs[3][...] = rows.astype(jnp.bfloat16)


def finish(chunks, hidden_ref, gain_ref, *refs):
    pieces, out_hbm, out_ref, sems = refs[:-3], refs[-3], refs[-2], refs[-1]
    width = hidden_ref.shape[1]
    x, y = lax.axis_index("x"), lax.axis_index("ctx")
    owners = ((x, y), (1 - x, y), (x, 1 - y), (1 - x, 1 - y))
    total = 0.0
    for piece in pieces:
        value = piece[...].astype(jnp.float32)
        total = total + jnp.sum(value * value, axis=-1, keepdims=True)
    scale = lax.rsqrt(total / width + norm_eps)
    start = 0
    copies = []
    for c, columns in enumerate(chunks):
        for i, (px, py) in enumerate(owners):
            at = pl.ds(pl.multiple_of((py * 2 + px) * (width // 4) + start, 128), columns)
            normed = pieces[c * 4 + i][...].astype(jnp.float32) * scale * gain_ref[:, at]
            out_ref[:, at] = (hidden_ref[:, at].astype(jnp.float32) + normed).astype(jnp.bfloat16)
            copies.append(
                pltpu.make_async_copy(out_ref.at[:, at], out_hbm.at[:, at], sems.at[c * 4 + i])
            )
            copies[-1].start()
        start += columns
    for copy in copies:
        copy.wait()


def shards(ring, chunks, hidden_rows, query_proj, key_proj, value_proj, order_pos, post_gain, out_weight):
    n = len(ring)
    tokens = query_proj.shape[1]
    width = hidden_rows.shape[2]
    swap = [(0, 1), (1, 0)]
    along = [(ring[i], ring[(i + 1) % n]) for i in range(n)]

    def over(value, axis):
        if axis == "diag":
            return lax.ppermute(value, ("ctx", "x"), [(i, 3 - i) for i in range(4)])
        return lax.ppermute(value, axis, along if axis == "z" else swap)

    rows, block = out_weight.shape
    quarter = block // 2

    def call(body, outs, ins, name, scratch=(), label=None):
        return pl.pallas_call(
            body,
            out_shape=outs,
            in_specs=[VMEM] * ins,
            out_specs=[VMEM] * len(outs),
            scratch_shapes=scratch,
            compiler_params=params(),
            cost_estimate=pl.CostEstimate(
                flops=int(COSTS.get(label or name, 0) * PER_CYCLE) + 1, bytes_accessed=0, transcendentals=0
            ),
            name=name,
        )

    moves, kernels = {}, {}
    kernels["cut"] = (call(cut, [bf16(rows, quarter)] * 2, 1, "cut"), ("w",), ("a0", "awayo"))
    kernels["stage"] = (
        call(
            stage,
            [bf16(tokens, a.shape[2]) for a in (query_proj, key_proj, value_proj)]
            + [jax.ShapeDtypeStruct(order_pos.shape, jnp.int32)],
            4,
            "stage",
        ),
        ("qo", "Ko", "Vo", "poso"),
        ("q", "Kq", "Vq", "posq"),
    )
    wide = bf16(tokens, HQ * DH // ACTS)
    halves = "12"[:ACTS]
    for k, axis in (("K", "ctx"), ("V", "ctx"), ("pos", "ctx"), ("B0", "x")):
        moves[k] = ({"B0": "awayo"}.get(k, k + "o"), axis)
    kernels["att"] = (
        call(attend, [wide] * ACTS, 7, "attend", label="att"),
        ("q", "Kq", "K", "Vq", "V", "posq", "pos"),
        tuple("h" + i for i in halves),
    )
    for i in halves:
        moves["x" + i] = ("h" + i, "x")
        moves["y" + i] = ("h" + i, "ctx")
    if ACTS == 2:
        moves["d1"], moves["d2"] = ("y1", "x"), ("x2", "ctx")
        acts = ("h1", "h2", "x1", "x2", "y1", "y2", "d1", "d2")
        sizes = (2, 2, 2, 2)
    else:
        half = bf16(tokens, HQ * DH // 2)
        kernels["hy"] = (call(functools.partial(part, 0), [half], 1, "halves", label="hy"), ("y1",), ("y1l",))
        kernels["hx"] = (call(functools.partial(part, 1), [half], 1, "halves", label="hx"), ("x1",), ("x1r",))
        moves["d1"], moves["d2"] = ("y1l", "x"), ("x1r", "ctx")
        acts, sizes = ("h1", "x1", "y1", "d1", "d2"), (1, 1, 1, 2)
    for chain, whole in WHOLE_STEPS.items():
        for i in range(1, whole + 1):
            moves[chain + str(i)] = (chain + str(i - 1), "z")
        if whole < n - 1:
            last = chain + str(whole)
            kernels["split" + chain] = (
                call(split, [bf16(rows, c) for c in chunks], 1, "split", label="split" + chain),
                (last,),
                tuple("%s_%d" % (last, c) for c in range(len(chunks))),
            )
    def spot(name):
        return name[0], int(name[1:])

    sure = [spot(name) for names in PACKS for name in names]
    late = [(chain, i) for chain in WHOLE_STEPS for i in range(n) if (chain, i) not in sure]
    order, bufs = [], []
    for k, names in enumerate(PACKS):
        kernels["pk%d" % k] = (
            call(stack, [bf16(len(names) * rows, quarter)], len(names), "stack", label="pk%d" % k),
            tuple(names),
            ("k%d" % k,),
        )
        moves["ck%d" % k] = ("k%d" % k, "core")
        bufs += ["k%d" % k, "ck%d" % k]
        for same in (True, False):
            order += [(spot(name)[1], name[0] == "a", same) for name in names]
    done = len(order)
    order += [(i, chain == "a", same) for chain, i in late for same in (True, False)]
    three = (*acts[: 3 * ACTS],)
    kernels["early"] = (
        call(
            functools.partial(early, ring, (ACTS,) * 3, order[:done]),
            [
                jax.ShapeDtypeStruct((3 * tokens, quarter), jnp.float32),
                bf16(3 * tokens, HQ * DH),
                bf16(done * DH, quarter),
            ],
            len(three) + len(bufs),
            "early",
        ),
        (*three, *bufs),
        ("acc", "aall", "wall"),
    )
    for c, columns in enumerate(chunks):
        j = str(c)
        bufs = []
        for chain, i in late:
            name = "%s%d" % (chain, i) if i <= WHOLE_STEPS[chain] else "%s%d_%d" % (chain, i, c)
            if i > WHOLE_STEPS[chain]:
                moves[name] = ("%s%d_%d" % (chain, i - 1, c), "z")
            moves["c" + name] = (name, "core")
            bufs += [name, "c" + name]
        operands = ("acc", "aall", "wall", *acts[3 * ACTS :], *bufs)
        results = tuple("p" + k + j for k in "oxyd")
        kernels["proj" + j] = (
            call(
                functools.partial(project, ring, sum(chunks[:c]), (2,), order),
                [bf16(tokens, columns)] * 4,
                len(operands),
                "project",
                [pltpu.VMEM((tokens, HQ * DH), jnp.bfloat16)],
                label="proj" + j,
            ),
            operands,
            results,
        )
        for k, axis in zip("xyd", ("x", "ctx", "diag")):
            moves["r" + k + j] = ("p" + k + j, axis)

    held = dict(
        w=out_weight, qo=query_proj[0], Ko=key_proj[0], Vo=value_proj[0], poso=order_pos
    )

    def after(value, deps):
        for dep in deps:
            token, held[dep] = lax.optimization_barrier((lax.create_token(), held[dep]))
            token, value = lax.optimization_barrier((token, value))
        return value

    pending = list(kernels) + list(moves)
    pending.sort(key=lambda name: FIRST.index(name) if name in FIRST else len(FIRST))
    while pending:
        for name in pending:
            sources, results = (moves[name][:1], (name,)) if name in moves else kernels[name][1:]
            deps = [d for d in TIES.get(name, ())]
            if all(k in held for k in (*sources, *deps)):
                break
        pending.remove(name)
        first = after(held[sources[0]], deps)
        if name in moves:
            held[name] = over(first, moves[name][1])
        else:
            out = kernels[name][0](first, *(held[k] for k in sources[1:]))
            held.update(zip(results, out))

    pieces = [held[("po" if k == "o" else "r" + k) + str(c)] for c in range(len(chunks)) for k in "oxyd"]

    out = pl.pallas_call(
        functools.partial(finish, chunks),
        out_shape=bf16(tokens, width),
        in_specs=[VMEM] * (2 + len(pieces)),
        out_specs=HBM,
        scratch_shapes=[
            pltpu.VMEM((tokens, width), jnp.bfloat16),
            pltpu.SemaphoreType.DMA((len(pieces),)),
        ],
        compiler_params=params(),
        cost_estimate=pl.CostEstimate(flops=1, bytes_accessed=0, transcendentals=0),
        name="finish",
    )(hidden_rows[0], post_gain.reshape(1, width), *pieces)
    return out[None]


def plain_shards(hidden_rows, query_proj, key_proj, value_proj, order_pos, post_gain, out_weight):
    tokens = query_proj.shape[1]
    groups = HQ // HK
    positions = lax.all_gather(order_pos, "ctx", axis=1, tiled=True)[0]
    weight_block = lax.all_gather(out_weight, "fsdp", axis=0, tiled=True)
    query = query_proj[0].reshape(tokens, HK, groups, DH)
    keys = lax.all_gather(key_proj, "ctx", axis=1, tiled=True)[0].reshape(-1, HK, DH)
    values = lax.all_gather(value_proj, "ctx", axis=1, tiled=True)[0].reshape(-1, HK, DH)
    scores = jnp.einsum("thgd,nhd->hgtn", query, keys, preferred_element_type=jnp.float32)
    capped = soft_cap * jnp.tanh(scores * score_scale / soft_cap)
    visible = positions[None, :] <= order_pos[0][:, None]
    weights = jnp.where(visible, jnp.exp(capped), 0.0)
    numerator = jnp.einsum(
        "hgtn,nhd->thgd", weights.astype(jnp.bfloat16), values, preferred_element_type=jnp.float32
    )
    denominator = jnp.transpose(jnp.sum(weights, axis=-1), (2, 0, 1))
    attended = (numerator / denominator[..., None]).astype(jnp.bfloat16).reshape(1, tokens, HQ * DH)
    projected = jnp.dot(
        lax.all_gather(attended, "ctx", axis=1, tiled=True)[0],
        weight_block,
        preferred_element_type=jnp.float32,
    )
    token_rows = lax.all_to_all(
        projected.astype(jnp.bfloat16), "ctx", split_axis=0, concat_axis=1, tiled=True
    ).astype(jnp.float32)
    mean = jnp.mean(token_rows * token_rows, axis=-1, keepdims=True)
    normed = token_rows * lax.rsqrt(mean + norm_eps) * post_gain
    return (hidden_rows[0].astype(jnp.float32) + normed).astype(jnp.bfloat16)[None]


def solution(mesh):
    ctx, fsdp = mesh.shape["ctx"], mesh.shape["fsdp"]
    rows = "fsdp"
    body = plain_shards
    if ctx == 2 and fsdp % 4 == 0 and fsdp == HQ:
        mesh = Mesh(np.asarray(mesh.devices).reshape(ctx, fsdp // 4, 2, 2), ("ctx", "z", "x", "core"))
        rows = ("z", "x", "core")
        body = functools.partial(shards, ring_of(fsdp // 4), CHUNKS)
    placed = (
        P(rows, "ctx", None),
        P(rows, "ctx", None),
        P(rows, "ctx", None),
        P(rows, "ctx", None),
        P(rows, "ctx"),
        P(),
        P(rows, "ctx"),
    )
    return jax.shard_map(
        body, mesh=mesh, in_specs=placed, out_specs=P(rows, "ctx", None), check_vma=False
    )
```

```python
import functools

import jax
import jax.numpy as jnp
import numpy as np
from jax import lax
from jax.experimental import pallas as pl
from jax.experimental.pallas import tpu as pltpu
from jax.sharding import Mesh
from jax.sharding import PartitionSpec as P

HQ = 16
HK = 8
DH = 128

score_scale = 1.0 / 12.0
soft_cap = 50.0
norm_eps = 1e-06

CHUNKS = (640, 512)
PACKS = (('a0', 'B0', 'a1', 'B1'), ('a2', 'B2'))
WHOLE_STEPS = {'a': 3, 'B': 2}
TIES = {'rd1': ('rd0',), 'ca3': ('ck0',), 'pos': ('a1',), 'hy': ('k1',)}
COSTS = {'splitB': 9000, 'hy': 1500, 'proj0': 1500, 'pk0': 9000, 'cut': 3000, 'early': 6000, 'att': 3000, 'pk1': 6000, 'hx': 9000}
PER_CYCLE = 524288
FIRST = ()
ACTS = 1
VMEM_LIMIT = 20 * 2**20
VMEM = pl.BlockSpec(memory_space=pltpu.VMEM)
HBM = pl.BlockSpec(memory_space=pl.ANY)


def params():
    return pltpu.CompilerParams(vmem_limit_bytes=VMEM_LIMIT)


def bf16(*dims):
    return jax.ShapeDtypeStruct(dims, jnp.bfloat16)


def ring_of(n):
    return list(range(0, 2, 1))[:1] + list(range(1, n, 2)) + list(range(2, n, 2))[::-1]


def cut(w_ref, near, away):
    quarter = near.shape[1]
    me = lax.axis_index("x")
    near[...] = w_ref[:, pl.ds(pl.multiple_of(me * quarter, 128), quarter)]
    away[...] = w_ref[:, pl.ds(pl.multiple_of((1 - me) * quarter, 128), quarter)]


def stage(*refs):
    half = len(refs) // 2
    for ref, out in zip(refs[:half], refs[half:]):
        out[...] = ref[...]


def split(ref, *outs):
    start = 0
    for out in outs:
        out[...] = ref[:, pl.ds(start, out.shape[1])]
        start += out.shape[1]


def attend(q_ref, k_own, k_far, v_own, v_far, pos_own, pos_far, *outs):
    tokens = q_ref.shape[0]
    groups = HQ // HK
    per = HQ // len(outs)
    own = pos_own[...].astype(jnp.float32)
    far = pos_far[...].astype(jnp.float32)
    mine = jnp.transpose(jnp.broadcast_to(own, (tokens, tokens)))[:, :1]
    visible = jnp.concatenate([own, far], axis=1) <= mine
    visible = jnp.concatenate([visible] * groups, axis=0)
    for head in range(HK):
        at = pl.ds(head * DH, DH)
        q_at = [pl.ds((head * groups + g) * DH, DH) for g in range(groups)]
        query = jnp.concatenate([q_ref[:, each] for each in q_at], axis=0)
        keys = jnp.concatenate([k_own[:, at], k_far[:, at]], axis=0)
        values = jnp.concatenate([v_own[:, at], v_far[:, at]], axis=0)
        scores = lax.dot_general(
            query, keys, (((1,), (1,)), ((), ())), preferred_element_type=jnp.float32
        )
        capped = soft_cap * jnp.tanh(scores * (score_scale / soft_cap))
        weights = jnp.where(visible, jnp.exp(capped), 0.0)
        total = jnp.sum(weights, axis=-1, keepdims=True)
        mixed = jnp.dot(weights.astype(jnp.bfloat16), values, preferred_element_type=jnp.float32)
        mixed = (mixed / total).astype(jnp.bfloat16)
        for g in range(groups):
            h = head * groups + g
            outs[h // per][:, pl.ds((h % per) * DH, DH)] = mixed[g * tokens : (g + 1) * tokens]


def head_of(step, same_x, same_core, ring):
    z, x, core = (lax.axis_index(name) for name in ("z", "x", "core"))
    n = len(ring)
    source = 0
    for i, stop in enumerate(ring):
        source = source + jnp.where(z == stop, ring[(i - step) % n], 0)
    x = x if same_x else 1 - x
    core = core if same_core else 1 - core
    return (source * 2 + x) * 2 + core


def part(which, ref, out):
    out[...] = ref[:, pl.ds(which * out.shape[1], out.shape[1])]


def stack(*refs):
    bufs, out = refs[:-1], refs[-1]
    for i, buf in enumerate(bufs):
        out[pl.ds(i * buf.shape[0], buf.shape[0]), :] = buf[...]


def stack_acts(sizes, acts, a_all):
    tokens = a_all.shape[0] // len(sizes)
    taken = 0
    for g, parts in enumerate(sizes):
        at = 0
        for act in acts[taken : taken + parts]:
            a_all[pl.ds(g * tokens, tokens), pl.ds(at, act.shape[1])] = act[...]
            at += act.shape[1]
        taken += parts


def columns_of(a_all, heads):
    return jnp.concatenate(
        [a_all[:, pl.ds(pl.multiple_of(head * DH, DH), DH)] for head in heads], axis=1
    )


def early(ring, sizes, heads, *refs):
    count = sum(sizes)
    acts, bufs, (acc, a_all, w_all) = refs[:count], refs[count:-3], refs[-3:]
    stack_acts(sizes, acts, a_all)
    at = 0
    for buf in bufs:
        w_all[pl.ds(at, buf.shape[0]), :] = buf[...]
        at += buf.shape[0]
    heads = [head_of(*head, ring) for head in heads]
    acc[...] = jnp.dot(columns_of(a_all, heads), w_all[...], preferred_element_type=jnp.float32)


def project(ring, first, sizes, heads, acc, a_all, w_all, *refs):
    count = sum(sizes)
    acts, bufs, outs, a_last = refs[:count], refs[count:-5], refs[-5:-1], refs[-1]
    tokens, columns = outs[0].shape
    done = w_all.shape[0] // DH
    stack_acts(sizes, acts, a_last)
    heads = [head_of(*head, ring) for head in heads]
    w_late = jnp.concatenate(
        [buf[:, pl.ds(0 if buf.shape[1] == columns else first, columns)] for buf in bufs], axis=0
    )
    rows = acc[:, pl.ds(first, columns)] + jnp.dot(
        columns_of(a_all, heads[done:]), w_late, preferred_element_type=jnp.float32
    )
    for g in range(3):
        outs[g][...] = rows[g * tokens : (g + 1) * tokens].astype(jnp.bfloat16)
    rows = jnp.dot(
        columns_of(a_last, heads[:done]),
        w_all[:, pl.ds(first, columns)],
        preferred_element_type=jnp.float32,
    ) + jnp.dot(columns_of(a_last, heads[done:]), w_late, preferred_element_type=jnp.float32)
    outs[3][...] = rows.astype(jnp.bfloat16)


def finish(chunks, hidden_ref, gain_ref, *refs):
    pieces, out_hbm, out_ref, sems = refs[:-3], refs[-3], refs[-2], refs[-1]
    width = hidden_ref.shape[1]
    x, y = lax.axis_index("x"), lax.axis_index("ctx")
    owners = ((x, y), (1 - x, y), (x, 1 - y), (1 - x, 1 - y))
    total = 0.0
    for piece in pieces:
        value = piece[...].astype(jnp.float32)
        total = total + jnp.sum(value * value, axis=-1, keepdims=True)
    scale = lax.rsqrt(total / width + norm_eps)
    start = 0
    copies = []
    for c, columns in enumerate(chunks):
        for i, (px, py) in enumerate(owners):
            at = pl.ds(pl.multiple_of((py * 2 + px) * (width // 4) + start, 128), columns)
            normed = pieces[c * 4 + i][...].astype(jnp.float32) * scale * gain_ref[:, at]
            out_ref[:, at] = (hidden_ref[:, at].astype(jnp.float32) + normed).astype(jnp.bfloat16)
            copies.append(
                pltpu.make_async_copy(out_ref.at[:, at], out_hbm.at[:, at], sems.at[c * 4 + i])
            )
            copies[-1].start()
        start += columns
    for copy in copies:
        copy.wait()


def shards(ring, chunks, hidden_rows, query_proj, key_proj, value_proj, order_pos, post_gain, out_weight):
    n = len(ring)
    tokens = query_proj.shape[1]
    width = hidden_rows.shape[2]
    swap = [(0, 1), (1, 0)]
    along = [(ring[i], ring[(i + 1) % n]) for i in range(n)]

    def over(value, axis):
        if axis == "diag":
            return lax.ppermute(value, ("ctx", "x"), [(i, 3 - i) for i in range(4)])
        return lax.ppermute(value, axis, along if axis == "z" else swap)

    rows, block = out_weight.shape
    quarter = block // 2

    def call(body, outs, ins, name, scratch=(), label=None):
        return pl.pallas_call(
            body,
            out_shape=outs,
            in_specs=[VMEM] * ins,
            out_specs=[VMEM] * len(outs),
            scratch_shapes=scratch,
            compiler_params=params(),
            cost_estimate=pl.CostEstimate(
                flops=int(COSTS.get(label or name, 0) * PER_CYCLE) + 1, bytes_accessed=0, transcendentals=0
            ),
            name=name,
        )

    moves, kernels = {}, {}
    kernels["cut"] = (call(cut, [bf16(rows, quarter)] * 2, 1, "cut"), ("w",), ("a0", "awayo"))
    kernels["stage"] = (
        call(
            stage,
            [bf16(tokens, a.shape[2]) for a in (query_proj, key_proj, value_proj)]
            + [jax.ShapeDtypeStruct(order_pos.shape, jnp.int32)],
            4,
            "stage",
        ),
        ("qo", "Ko", "Vo", "poso"),
        ("q", "Kq", "Vq", "posq"),
    )
    wide = bf16(tokens, HQ * DH // ACTS)
    halves = "12"[:ACTS]
    for k, axis in (("K", "ctx"), ("V", "ctx"), ("pos", "ctx"), ("B0", "x")):
        moves[k] = ({"B0": "awayo"}.get(k, k + "o"), axis)
    kernels["att"] = (
        call(attend, [wide] * ACTS, 7, "attend", label="att"),
        ("q", "Kq", "K", "Vq", "V", "posq", "pos"),
        tuple("h" + i for i in halves),
    )
    for i in halves:
        moves["x" + i] = ("h" + i, "x")
        moves["y" + i] = ("h" + i, "ctx")
    if ACTS == 2:
        moves["d1"], moves["d2"] = ("y1", "x"), ("x2", "ctx")
        acts = ("h1", "h2", "x1", "x2", "y1", "y2", "d1", "d2")
        sizes = (2, 2, 2, 2)
    else:
        half = bf16(tokens, HQ * DH // 2)
        kernels["hy"] = (call(functools.partial(part, 0), [half], 1, "halves", label="hy"), ("y1",), ("y1l",))
        kernels["hx"] = (call(functools.partial(part, 1), [half], 1, "halves", label="hx"), ("x1",), ("x1r",))
        moves["d1"], moves["d2"] = ("y1l", "x"), ("x1r", "ctx")
        acts, sizes = ("h1", "x1", "y1", "d1", "d2"), (1, 1, 1, 2)
    for chain, whole in WHOLE_STEPS.items():
        for i in range(1, whole + 1):
            moves[chain + str(i)] = (chain + str(i - 1), "z")
        if whole < n - 1:
            last = chain + str(whole)
            kernels["split" + chain] = (
                call(split, [bf16(rows, c) for c in chunks], 1, "split", label="split" + chain),
                (last,),
                tuple("%s_%d" % (last, c) for c in range(len(chunks))),
            )
    def spot(name):
        return name[0], int(name[1:])

    sure = [spot(name) for names in PACKS for name in names]
    late = [(chain, i) for chain in WHOLE_STEPS for i in range(n) if (chain, i) not in sure]
    order, bufs = [], []
    for k, names in enumerate(PACKS):
        kernels["pk%d" % k] = (
            call(stack, [bf16(len(names) * rows, quarter)], len(names), "stack", label="pk%d" % k),
            tuple(names),
            ("k%d" % k,),
        )
        moves["ck%d" % k] = ("k%d" % k, "core")
        bufs += ["k%d" % k, "ck%d" % k]
        for same in (True, False):
            order += [(spot(name)[1], name[0] == "a", same) for name in names]
    done = len(order)
    order += [(i, chain == "a", same) for chain, i in late for same in (True, False)]
    three = (*acts[: 3 * ACTS],)
    kernels["early"] = (
        call(
            functools.partial(early, ring, (ACTS,) * 3, order[:done]),
            [
                jax.ShapeDtypeStruct((3 * tokens, quarter), jnp.float32),
                bf16(3 * tokens, HQ * DH),
                bf16(done * DH, quarter),
            ],
            len(three) + len(bufs),
            "early",
        ),
        (*three, *bufs),
        ("acc", "aall", "wall"),
    )
    for c, columns in enumerate(chunks):
        j = str(c)
        bufs = []
        for chain, i in late:
            name = "%s%d" % (chain, i) if i <= WHOLE_STEPS[chain] else "%s%d_%d" % (chain, i, c)
            if i > WHOLE_STEPS[chain]:
                moves[name] = ("%s%d_%d" % (chain, i - 1, c), "z")
            moves["c" + name] = (name, "core")
            bufs += [name, "c" + name]
        operands = ("acc", "aall", "wall", *acts[3 * ACTS :], *bufs)
        results = tuple("p" + k + j for k in "oxyd")
        kernels["proj" + j] = (
            call(
                functools.partial(project, ring, sum(chunks[:c]), (2,), order),
                [bf16(tokens, columns)] * 4,
                len(operands),
                "project",
                [pltpu.VMEM((tokens, HQ * DH), jnp.bfloat16)],
                label="proj" + j,
            ),
            operands,
            results,
        )
        for k, axis in zip("xyd", ("x", "ctx", "diag")):
            moves["r" + k + j] = ("p" + k + j, axis)

    held = dict(
        w=out_weight, qo=query_proj[0], Ko=key_proj[0], Vo=value_proj[0], poso=order_pos
    )

    def after(value, deps):
        for dep in deps:
            token, held[dep] = lax.optimization_barrier((lax.create_token(), held[dep]))
            token, value = lax.optimization_barrier((token, value))
        return value

    pending = list(kernels) + list(moves)
    pending.sort(key=lambda name: FIRST.index(name) if name in FIRST else len(FIRST))
    while pending:
        for name in pending:
            sources, results = (moves[name][:1], (name,)) if name in moves else kernels[name][1:]
            deps = [d for d in TIES.get(name, ())]
            if all(k in held for k in (*sources, *deps)):
                break
        pending.remove(name)
        first = after(held[sources[0]], deps)
        if name in moves:
            held[name] = over(first, moves[name][1])
        else:
            out = kernels[name][0](first, *(held[k] for k in sources[1:]))
            held.update(zip(results, out))

    pieces = [held[("po" if k == "o" else "r" + k) + str(c)] for c in range(len(chunks)) for k in "oxyd"]

    out = pl.pallas_call(
        functools.partial(finish, chunks),
        out_shape=bf16(tokens, width),
        in_specs=[VMEM] * (2 + len(pieces)),
        out_specs=HBM,
        scratch_shapes=[
            pltpu.VMEM((tokens, width), jnp.bfloat16),
            pltpu.SemaphoreType.DMA((len(pieces),)),
        ],
        compiler_params=params(),
        cost_estimate=pl.CostEstimate(flops=1, bytes_accessed=0, transcendentals=0),
        name="finish",
    )(hidden_rows[0], post_gain.reshape(1, width), *pieces)
    return out[None]


def plain_shards(hidden_rows, query_proj, key_proj, value_proj, order_pos, post_gain, out_weight):
    tokens = query_proj.shape[1]
    groups = HQ // HK
    positions = lax.all_gather(order_pos, "ctx", axis=1, tiled=True)[0]
    weight_block = lax.all_gather(out_weight, "fsdp", axis=0, tiled=True)
    query = query_proj[0].reshape(tokens, HK, groups, DH)
    keys = lax.all_gather(key_proj, "ctx", axis=1, tiled=True)[0].reshape(-1, HK, DH)
    values = lax.all_gather(value_proj, "ctx", axis=1, tiled=True)[0].reshape(-1, HK, DH)
    scores = jnp.einsum("thgd,nhd->hgtn", query, keys, preferred_element_type=jnp.float32)
    capped = soft_cap * jnp.tanh(scores * score_scale / soft_cap)
    visible = positions[None, :] <= order_pos[0][:, None]
    weights = jnp.where(visible, jnp.exp(capped), 0.0)
    numerator = jnp.einsum(
        "hgtn,nhd->thgd", weights.astype(jnp.bfloat16), values, preferred_element_type=jnp.float32
    )
    denominator = jnp.transpose(jnp.sum(weights, axis=-1), (2, 0, 1))
    attended = (numerator / denominator[..., None]).astype(jnp.bfloat16).reshape(1, tokens, HQ * DH)
    projected = jnp.dot(
        lax.all_gather(attended, "ctx", axis=1, tiled=True)[0],
        weight_block,
        preferred_element_type=jnp.float32,
    )
    token_rows = lax.all_to_all(
        projected.astype(jnp.bfloat16), "ctx", split_axis=0, concat_axis=1, tiled=True
    ).astype(jnp.float32)
    mean = jnp.mean(token_rows * token_rows, axis=-1, keepdims=True)
    normed = token_rows * lax.rsqrt(mean + norm_eps) * post_gain
    return (hidden_rows[0].astype(jnp.float32) + normed).astype(jnp.bfloat16)[None]


def solution(mesh):
    ctx, fsdp = mesh.shape["ctx"], mesh.shape["fsdp"]
    rows = "fsdp"
    body = plain_shards
    if ctx == 2 and fsdp % 4 == 0 and fsdp == HQ:
        mesh = Mesh(np.asarray(mesh.devices).reshape(ctx, fsdp // 4, 2, 2), ("ctx", "z", "x", "core"))
        rows = ("z", "x", "core")
        body = functools.partial(shards, ring_of(fsdp // 4), CHUNKS)
    placed = (
        P(rows, "ctx", None),
        P(rows, "ctx", None),
        P(rows, "ctx", None),
        P(rows, "ctx", None),
        P(rows, "ctx"),
        P(),
        P(rows, "ctx"),
    )
    return jax.shard_map(
        body, mesh=mesh, in_specs=placed, out_specs=P(rows, "ctx", None), check_vma=False
    )
```

```python
import functools

import jax
import jax.numpy as jnp
import numpy as np
from jax import lax
from jax.experimental import pallas as pl
from jax.experimental.pallas import tpu as pltpu
from jax.sharding import Mesh
from jax.sharding import PartitionSpec as P

HQ = 16
HK = 8
DH = 128

score_scale = 1.0 / 12.0
soft_cap = 50.0
norm_eps = 1e-06

CHUNKS = (640, 512)
PACKS = (('a0', 'B0', 'a1', 'B1'), ('a2', 'B2'))
WHOLE_STEPS = {'a': 3, 'B': 2}
TIES = {'rd1': ('rd0',), 'ca3': ('ck1',), 'pos': ('a1',), 'hy': ('k1',), 'B3_0': ('y1l',)}
COSTS = {'splitB': 9000, 'hy': 1500, 'proj0': 1500, 'pk0': 9000, 'cut': 3000, 'early': 6000, 'att': 3000, 'pk1': 6000, 'hx': 12000}
PER_CYCLE = 524288
FIRST = ()
ACTS = 1
VMEM_LIMIT = 20 * 2**20
VMEM = pl.BlockSpec(memory_space=pltpu.VMEM)
HBM = pl.BlockSpec(memory_space=pl.ANY)


def params():
    return pltpu.CompilerParams(vmem_limit_bytes=VMEM_LIMIT)


def bf16(*dims):
    return jax.ShapeDtypeStruct(dims, jnp.bfloat16)


def ring_of(n):
    return list(range(0, 2, 1))[:1] + list(range(1, n, 2)) + list(range(2, n, 2))[::-1]


def cut(w_ref, near, away):
    quarter = near.shape[1]
    me = lax.axis_index("x")
    near[...] = w_ref[:, pl.ds(pl.multiple_of(me * quarter, 128), quarter)]
    away[...] = w_ref[:, pl.ds(pl.multiple_of((1 - me) * quarter, 128), quarter)]


def stage(*refs):
    half = len(refs) // 2
    for ref, out in zip(refs[:half], refs[half:]):
        out[...] = ref[...]


def split(ref, *outs):
    start = 0
    for out in outs:
        out[...] = ref[:, pl.ds(start, out.shape[1])]
        start += out.shape[1]


def attend(q_ref, k_own, k_far, v_own, v_far, pos_own, pos_far, *outs):
    tokens = q_ref.shape[0]
    groups = HQ // HK
    per = HQ // len(outs)
    own = pos_own[...].astype(jnp.float32)
    far = pos_far[...].astype(jnp.float32)
    mine = jnp.transpose(jnp.broadcast_to(own, (tokens, tokens)))[:, :1]
    visible = jnp.concatenate([own, far], axis=1) <= mine
    visible = jnp.concatenate([visible] * groups, axis=0)
    for head in range(HK):
        at = pl.ds(head * DH, DH)
        q_at = [pl.ds((head * groups + g) * DH, DH) for g in range(groups)]
        query = jnp.concatenate([q_ref[:, each] for each in q_at], axis=0)
        keys = jnp.concatenate([k_own[:, at], k_far[:, at]], axis=0)
        values = jnp.concatenate([v_own[:, at], v_far[:, at]], axis=0)
        scores = lax.dot_general(
            query, keys, (((1,), (1,)), ((), ())), preferred_element_type=jnp.float32
        )
        capped = soft_cap * jnp.tanh(scores * (score_scale / soft_cap))
        weights = jnp.where(visible, jnp.exp(capped), 0.0)
        total = jnp.sum(weights, axis=-1, keepdims=True)
        mixed = jnp.dot(weights.astype(jnp.bfloat16), values, preferred_element_type=jnp.float32)
        mixed = (mixed / total).astype(jnp.bfloat16)
        for g in range(groups):
            h = head * groups + g
            outs[h // per][:, pl.ds((h % per) * DH, DH)] = mixed[g * tokens : (g + 1) * tokens]


def head_of(step, same_x, same_core, ring):
    z, x, core = (lax.axis_index(name) for name in ("z", "x", "core"))
    n = len(ring)
    source = 0
    for i, stop in enumerate(ring):
        source = source + jnp.where(z == stop, ring[(i - step) % n], 0)
    x = x if same_x else 1 - x
    core = core if same_core else 1 - core
    return (source * 2 + x) * 2 + core


def part(which, ref, out):
    out[...] = ref[:, pl.ds(which * out.shape[1], out.shape[1])]


def stack(*refs):
    bufs, out = refs[:-1], refs[-1]
    for i, buf in enumerate(bufs):
        out[pl.ds(i * buf.shape[0], buf.shape[0]), :] = buf[...]


def stack_acts(sizes, acts, a_all):
    tokens = a_all.shape[0] // len(sizes)
    taken = 0
    for g, parts in enumerate(sizes):
        at = 0
        for act in acts[taken : taken + parts]:
            a_all[pl.ds(g * tokens, tokens), pl.ds(at, act.shape[1])] = act[...]
            at += act.shape[1]
        taken += parts


def columns_of(a_all, heads):
    return jnp.concatenate(
        [a_all[:, pl.ds(pl.multiple_of(head * DH, DH), DH)] for head in heads], axis=1
    )


def early(ring, sizes, heads, *refs):
    count = sum(sizes)
    acts, bufs, (acc, a_all, w_all) = refs[:count], refs[count:-3], refs[-3:]
    stack_acts(sizes, acts, a_all)
    at = 0
    for buf in bufs:
        w_all[pl.ds(at, buf.shape[0]), :] = buf[...]
        at += buf.shape[0]
    heads = [head_of(*head, ring) for head in heads]
    acc[...] = jnp.dot(columns_of(a_all, heads), w_all[...], preferred_element_type=jnp.float32)


def project(ring, first, sizes, heads, acc, a_all, w_all, *refs):
    count = sum(sizes)
    acts, bufs, outs, a_last = refs[:count], refs[count:-5], refs[-5:-1], refs[-1]
    tokens, columns = outs[0].shape
    done = w_all.shape[0] // DH
    stack_acts(sizes, acts, a_last)
    heads = [head_of(*head, ring) for head in heads]
    w_late = jnp.concatenate(
        [buf[:, pl.ds(0 if buf.shape[1] == columns else first, columns)] for buf in bufs], axis=0
    )
    rows = acc[:, pl.ds(first, columns)] + jnp.dot(
        columns_of(a_all, heads[done:]), w_late, preferred_element_type=jnp.float32
    )
    for g in range(3):
        outs[g][...] = rows[g * tokens : (g + 1) * tokens].astype(jnp.bfloat16)
    rows = jnp.dot(
        columns_of(a_last, heads[:done]),
        w_all[:, pl.ds(first, columns)],
        preferred_element_type=jnp.float32,
    ) + jnp.dot(columns_of(a_last, heads[done:]), w_late, preferred_element_type=jnp.float32)
    outs[3][...] = rows.astype(jnp.bfloat16)


def finish(chunks, hidden_ref, gain_ref, *refs):
    pieces, out_hbm, out_ref, sems = refs[:-3], refs[-3], refs[-2], refs[-1]
    rows, width = hidden_ref.shape
    x, y = lax.axis_index("x"), lax.axis_index("ctx")
    owners = ((x, y), (1 - x, y), (x, 1 - y), (1 - x, 1 - y))
    places = []
    start = 0
    for columns in chunks:
        for px, py in owners:
            places.append(
                pl.ds(pl.multiple_of((py * 2 + px) * (width // 4) + start, 128), columns)
            )
        start += columns
    copies = []
    step = 16
    for i, top in enumerate(range(0, rows, step)):
        block = pl.ds(top, step)
        squares = jnp.zeros((step, 128), jnp.float32)
        for piece in pieces:
            for at in range(0, piece.shape[1], 128):
                value = piece[block, pl.ds(at, 128)].astype(jnp.float32)
                squares = squares + value * value
        scale = lax.rsqrt(jnp.sum(squares, axis=-1, keepdims=True) / width + norm_eps)
        for piece, at in zip(pieces, places):
            normed = piece[block, :].astype(jnp.float32) * scale * gain_ref[:, at]
            out_ref[block, at] = (hidden_ref[block, at].astype(jnp.float32) + normed).astype(
                jnp.bfloat16
            )
        copies.append(pltpu.make_async_copy(out_ref.at[block], out_hbm.at[block], sems.at[i]))
        copies[-1].start()
    for copy in copies:
        copy.wait()


def shards(ring, chunks, hidden_rows, query_proj, key_proj, value_proj, order_pos, post_gain, out_weight):
    n = len(ring)
    tokens = query_proj.shape[1]
    width = hidden_rows.shape[2]
    swap = [(0, 1), (1, 0)]
    along = [(ring[i], ring[(i + 1) % n]) for i in range(n)]

    def over(value, axis):
        if axis == "diag":
            return lax.ppermute(value, ("ctx", "x"), [(i, 3 - i) for i in range(4)])
        return lax.ppermute(value, axis, along if axis == "z" else swap)

    rows, block = out_weight.shape
    quarter = block // 2

    def call(body, outs, ins, name, scratch=(), label=None):
        return pl.pallas_call(
            body,
            out_shape=outs,
            in_specs=[VMEM] * ins,
            out_specs=[VMEM] * len(outs),
            scratch_shapes=scratch,
            compiler_params=params(),
            cost_estimate=pl.CostEstimate(
                flops=int(COSTS.get(label or name, 0) * PER_CYCLE) + 1, bytes_accessed=0, transcendentals=0
            ),
            name=name,
        )

    moves, kernels = {}, {}
    kernels["cut"] = (call(cut, [bf16(rows, quarter)] * 2, 1, "cut"), ("w",), ("a0", "awayo"))
    kernels["stage"] = (
        call(
            stage,
            [bf16(tokens, a.shape[2]) for a in (query_proj, key_proj, value_proj)]
            + [jax.ShapeDtypeStruct(order_pos.shape, jnp.int32)],
            4,
            "stage",
        ),
        ("qo", "Ko", "Vo", "poso"),
        ("q", "Kq", "Vq", "posq"),
    )
    wide = bf16(tokens, HQ * DH // ACTS)
    halves = "12"[:ACTS]
    for k, axis in (("K", "ctx"), ("V", "ctx"), ("pos", "ctx"), ("B0", "x")):
        moves[k] = ({"B0": "awayo"}.get(k, k + "o"), axis)
    kernels["att"] = (
        call(attend, [wide] * ACTS, 7, "attend", label="att"),
        ("q", "Kq", "K", "Vq", "V", "posq", "pos"),
        tuple("h" + i for i in halves),
    )
    for i in halves:
        moves["x" + i] = ("h" + i, "x")
        moves["y" + i] = ("h" + i, "ctx")
    if ACTS == 2:
        moves["d1"], moves["d2"] = ("y1", "x"), ("x2", "ctx")
        acts = ("h1", "h2", "x1", "x2", "y1", "y2", "d1", "d2")
        sizes = (2, 2, 2, 2)
    else:
        half = bf16(tokens, HQ * DH // 2)
        kernels["hy"] = (call(functools.partial(part, 0), [half], 1, "halves", label="hy"), ("y1",), ("y1l",))
        kernels["hx"] = (call(functools.partial(part, 1), [half], 1, "halves", label="hx"), ("x1",), ("x1r",))
        moves["d1"], moves["d2"] = ("y1l", "x"), ("x1r", "ctx")
        acts, sizes = ("h1", "x1", "y1", "d1", "d2"), (1, 1, 1, 2)
    for chain, whole in WHOLE_STEPS.items():
        for i in range(1, whole + 1):
            moves[chain + str(i)] = (chain + str(i - 1), "z")
        if whole < n - 1:
            last = chain + str(whole)
            kernels["split" + chain] = (
                call(split, [bf16(rows, c) for c in chunks], 1, "split", label="split" + chain),
                (last,),
                tuple("%s_%d" % (last, c) for c in range(len(chunks))),
            )
    def spot(name):
        return name[0], int(name[1:])

    sure = [spot(name) for names in PACKS for name in names]
    late = [(chain, i) for chain in WHOLE_STEPS for i in range(n) if (chain, i) not in sure]
    order, bufs = [], []
    for k, names in enumerate(PACKS):
        kernels["pk%d" % k] = (
            call(stack, [bf16(len(names) * rows, quarter)], len(names), "stack", label="pk%d" % k),
            tuple(names),
            ("k%d" % k,),
        )
        moves["ck%d" % k] = ("k%d" % k, "core")
        bufs += ["k%d" % k, "ck%d" % k]
        for same in (True, False):
            order += [(spot(name)[1], name[0] == "a", same) for name in names]
    done = len(order)
    order += [(i, chain == "a", same) for chain, i in late for same in (True, False)]
    three = (*acts[: 3 * ACTS],)
    kernels["early"] = (
        call(
            functools.partial(early, ring, (ACTS,) * 3, order[:done]),
            [
                jax.ShapeDtypeStruct((3 * tokens, quarter), jnp.float32),
                bf16(3 * tokens, HQ * DH),
                bf16(done * DH, quarter),
            ],
            len(three) + len(bufs),
            "early",
        ),
        (*three, *bufs),
        ("acc", "aall", "wall"),
    )
    for c, columns in enumerate(chunks):
        j = str(c)
        bufs = []
        for chain, i in late:
            name = "%s%d" % (chain, i) if i <= WHOLE_STEPS[chain] else "%s%d_%d" % (chain, i, c)
            if i > WHOLE_STEPS[chain]:
                moves[name] = ("%s%d_%d" % (chain, i - 1, c), "z")
            moves["c" + name] = (name, "core")
            bufs += [name, "c" + name]
        operands = ("acc", "aall", "wall", *acts[3 * ACTS :], *bufs)
        results = tuple("p" + k + j for k in "oxyd")
        kernels["proj" + j] = (
            call(
                functools.partial(project, ring, sum(chunks[:c]), (2,), order),
                [bf16(tokens, columns)] * 4,
                len(operands),
                "project",
                [pltpu.VMEM((tokens, HQ * DH), jnp.bfloat16)],
                label="proj" + j,
            ),
            operands,
            results,
        )
        for k, axis in zip("xyd", ("x", "ctx", "diag")):
            moves["r" + k + j] = ("p" + k + j, axis)

    held = dict(
        w=out_weight, qo=query_proj[0], Ko=key_proj[0], Vo=value_proj[0], poso=order_pos
    )

    def after(value, deps):
        for dep in deps:
            token, held[dep] = lax.optimization_barrier((lax.create_token(), held[dep]))
            token, value = lax.optimization_barrier((token, value))
        return value

    pending = list(kernels) + list(moves)
    pending.sort(key=lambda name: FIRST.index(name) if name in FIRST else len(FIRST))
    while pending:
        for name in pending:
            sources, results = (moves[name][:1], (name,)) if name in moves else kernels[name][1:]
            deps = [d for d in TIES.get(name, ())]
            if all(k in held for k in (*sources, *deps)):
                break
        pending.remove(name)
        first = after(held[sources[0]], deps)
        if name in moves:
            held[name] = over(first, moves[name][1])
        else:
            out = kernels[name][0](first, *(held[k] for k in sources[1:]))
            held.update(zip(results, out))

    pieces = [held[("po" if k == "o" else "r" + k) + str(c)] for c in range(len(chunks)) for k in "oxyd"]

    out = pl.pallas_call(
        functools.partial(finish, chunks),
        out_shape=bf16(tokens, width),
        in_specs=[VMEM] * (2 + len(pieces)),
        out_specs=HBM,
        scratch_shapes=[
            pltpu.VMEM((tokens, width), jnp.bfloat16),
            pltpu.SemaphoreType.DMA((tokens // 16,)),
        ],
        compiler_params=params(),
        cost_estimate=pl.CostEstimate(flops=1, bytes_accessed=0, transcendentals=0),
        name="finish",
    )(hidden_rows[0], post_gain.reshape(1, width), *pieces)
    return out[None]


def plain_shards(hidden_rows, query_proj, key_proj, value_proj, order_pos, post_gain, out_weight):
    tokens = query_proj.shape[1]
    groups = HQ // HK
    positions = lax.all_gather(order_pos, "ctx", axis=1, tiled=True)[0]
    weight_block = lax.all_gather(out_weight, "fsdp", axis=0, tiled=True)
    query = query_proj[0].reshape(tokens, HK, groups, DH)
    keys = lax.all_gather(key_proj, "ctx", axis=1, tiled=True)[0].reshape(-1, HK, DH)
    values = lax.all_gather(value_proj, "ctx", axis=1, tiled=True)[0].reshape(-1, HK, DH)
    scores = jnp.einsum("thgd,nhd->hgtn", query, keys, preferred_element_type=jnp.float32)
    capped = soft_cap * jnp.tanh(scores * score_scale / soft_cap)
    visible = positions[None, :] <= order_pos[0][:, None]
    weights = jnp.where(visible, jnp.exp(capped), 0.0)
    numerator = jnp.einsum(
        "hgtn,nhd->thgd", weights.astype(jnp.bfloat16), values, preferred_element_type=jnp.float32
    )
    denominator = jnp.transpose(jnp.sum(weights, axis=-1), (2, 0, 1))
    attended = (numerator / denominator[..., None]).astype(jnp.bfloat16).reshape(1, tokens, HQ * DH)
    projected = jnp.dot(
        lax.all_gather(attended, "ctx", axis=1, tiled=True)[0],
        weight_block,
        preferred_element_type=jnp.float32,
    )
    token_rows = lax.all_to_all(
        projected.astype(jnp.bfloat16), "ctx", split_axis=0, concat_axis=1, tiled=True
    ).astype(jnp.float32)
    mean = jnp.mean(token_rows * token_rows, axis=-1, keepdims=True)
    normed = token_rows * lax.rsqrt(mean + norm_eps) * post_gain
    return (hidden_rows[0].astype(jnp.float32) + normed).astype(jnp.bfloat16)[None]


def solution(mesh):
    ctx, fsdp = mesh.shape["ctx"], mesh.shape["fsdp"]
    rows = "fsdp"
    body = plain_shards
    if ctx == 2 and fsdp % 4 == 0 and fsdp == HQ:
        mesh = Mesh(np.asarray(mesh.devices).reshape(ctx, fsdp // 4, 2, 2), ("ctx", "z", "x", "core"))
        rows = ("z", "x", "core")
        body = functools.partial(shards, ring_of(fsdp // 4), CHUNKS)
    placed = (
        P(rows, "ctx", None),
        P(rows, "ctx", None),
        P(rows, "ctx", None),
        P(rows, "ctx", None),
        P(rows, "ctx"),
        P(),
        P(rows, "ctx"),
    )
    return jax.shard_map(
        body, mesh=mesh, in_specs=placed, out_specs=P(rows, "ctx", None), check_vma=False
    )
```

```python
import functools

import jax
import jax.numpy as jnp
import numpy as np
from jax import lax
from jax.experimental import pallas as pl
from jax.experimental.pallas import tpu as pltpu
from jax.sharding import Mesh
from jax.sharding import PartitionSpec as P

HQ = 16
HK = 8
DH = 128

score_scale = 1.0 / 12.0
soft_cap = 50.0
norm_eps = 1e-06

CHUNKS = (640, 512)
PACKS = (('a0', 'B0', 'a1', 'B1'), ('a2', 'B2'))
WHOLE_STEPS = {'a': 3, 'B': 2}
TIES = {'rd1': ('rd0',), 'ca3': ('ck1',), 'pos': ('a1',), 'hy': ('k1',), 'B3_0': ('y1l',)}
COSTS = {'splitB': 9000, 'hy': 1500, 'proj0': 1500, 'pk0': 9000, 'cut': 3000, 'early': 6000, 'att': 3000, 'pk1': 6000, 'hx': 9000}
PER_CYCLE = 524288
ACTS = 1
VMEM_LIMIT = 20 * 2**20
VMEM = pl.BlockSpec(memory_space=pltpu.VMEM)
HBM = pl.BlockSpec(memory_space=pl.ANY)


def params():
    return pltpu.CompilerParams(vmem_limit_bytes=VMEM_LIMIT)


def bf16(*dims):
    return jax.ShapeDtypeStruct(dims, jnp.bfloat16)


def ring_of(n):
    return list(range(0, 2, 1))[:1] + list(range(1, n, 2)) + list(range(2, n, 2))[::-1]


def cut(w_ref, near, away):
    quarter = near.shape[1]
    me = lax.axis_index("x")
    near[...] = w_ref[:, pl.ds(pl.multiple_of(me * quarter, 128), quarter)]
    away[...] = w_ref[:, pl.ds(pl.multiple_of((1 - me) * quarter, 128), quarter)]


def stage(*refs):
    half = len(refs) // 2
    for ref, out in zip(refs[:half], refs[half:]):
        out[...] = ref[...]


def split(ref, *outs):
    start = 0
    for out in outs:
        out[...] = ref[:, pl.ds(start, out.shape[1])]
        start += out.shape[1]


def attend(q_ref, k_own, k_far, v_own, v_far, pos_own, pos_far, *outs):
    tokens = q_ref.shape[0]
    groups = HQ // HK
    per = HQ // len(outs)
    own = pos_own[...].astype(jnp.float32)
    far = pos_far[...].astype(jnp.float32)
    mine = jnp.transpose(jnp.broadcast_to(own, (tokens, tokens)))[:, :1]
    visible = jnp.concatenate([own, far], axis=1) <= mine
    visible = jnp.concatenate([visible] * groups, axis=0)
    for head in range(HK):
        at = pl.ds(head * DH, DH)
        q_at = [pl.ds((head * groups + g) * DH, DH) for g in range(groups)]
        query = jnp.concatenate([q_ref[:, each] for each in q_at], axis=0)
        keys = jnp.concatenate([k_own[:, at], k_far[:, at]], axis=0)
        values = jnp.concatenate([v_own[:, at], v_far[:, at]], axis=0)
        scores = lax.dot_general(
            query, keys, (((1,), (1,)), ((), ())), preferred_element_type=jnp.float32
        )
        capped = soft_cap * jnp.tanh(scores * (score_scale / soft_cap))
        weights = jnp.where(visible, jnp.exp(capped), 0.0)
        total = jnp.sum(weights, axis=-1, keepdims=True)
        mixed = jnp.dot(weights.astype(jnp.bfloat16), values, preferred_element_type=jnp.float32)
        mixed = (mixed / total).astype(jnp.bfloat16)
        for g in range(groups):
            h = head * groups + g
            outs[h // per][:, pl.ds((h % per) * DH, DH)] = mixed[g * tokens : (g + 1) * tokens]


def head_of(step, same_x, same_core, ring):
    z, x, core = (lax.axis_index(name) for name in ("z", "x", "core"))
    n = len(ring)
    source = 0
    for i, stop in enumerate(ring):
        source = source + jnp.where(z == stop, ring[(i - step) % n], 0)
    x = x if same_x else 1 - x
    core = core if same_core else 1 - core
    return (source * 2 + x) * 2 + core


def part(which, ref, out):
    out[...] = ref[:, pl.ds(which * out.shape[1], out.shape[1])]


def stack(*refs):
    bufs, out = refs[:-1], refs[-1]
    for i, buf in enumerate(bufs):
        out[pl.ds(i * buf.shape[0], buf.shape[0]), :] = buf[...]


def stack_acts(sizes, acts, a_all):
    tokens = a_all.shape[0] // len(sizes)
    taken = 0
    for g, parts in enumerate(sizes):
        at = 0
        for act in acts[taken : taken + parts]:
            a_all[pl.ds(g * tokens, tokens), pl.ds(at, act.shape[1])] = act[...]
            at += act.shape[1]
        taken += parts


def columns_of(a_all, heads):
    return jnp.concatenate(
        [a_all[:, pl.ds(pl.multiple_of(head * DH, DH), DH)] for head in heads], axis=1
    )


def early(ring, sizes, heads, *refs):
    count = sum(sizes)
    acts, bufs, (acc, a_all, w_all) = refs[:count], refs[count:-3], refs[-3:]
    stack_acts(sizes, acts, a_all)
    at = 0
    for buf in bufs:
        w_all[pl.ds(at, buf.shape[0]), :] = buf[...]
        at += buf.shape[0]
    heads = [head_of(*head, ring) for head in heads]
    acc[...] = jnp.dot(columns_of(a_all, heads), w_all[...], preferred_element_type=jnp.float32)


def project(ring, first, sizes, heads, acc, a_all, w_all, *refs):
    count = sum(sizes)
    acts, bufs, outs, a_last = refs[:count], refs[count:-5], refs[-5:-1], refs[-1]
    tokens, columns = outs[0].shape
    done = w_all.shape[0] // DH
    stack_acts(sizes, acts, a_last)
    heads = [head_of(*head, ring) for head in heads]
    w_late = jnp.concatenate(
        [buf[:, pl.ds(0 if buf.shape[1] == columns else first, columns)] for buf in bufs], axis=0
    )
    rows = acc[:, pl.ds(first, columns)] + jnp.dot(
        columns_of(a_all, heads[done:]), w_late, preferred_element_type=jnp.float32
    )
    for g in range(3):
        outs[g][...] = rows[g * tokens : (g + 1) * tokens].astype(jnp.bfloat16)
    rows = jnp.dot(
        columns_of(a_last, heads[:done]),
        w_all[:, pl.ds(first, columns)],
        preferred_element_type=jnp.float32,
    ) + jnp.dot(columns_of(a_last, heads[done:]), w_late, preferred_element_type=jnp.float32)
    outs[3][...] = rows.astype(jnp.bfloat16)


def finish(chunks, hidden_ref, gain_ref, *refs):
    pieces, out_hbm, out_ref, sems = refs[:-3], refs[-3], refs[-2], refs[-1]
    rows, width = hidden_ref.shape
    x, y = lax.axis_index("x"), lax.axis_index("ctx")
    owners = ((x, y), (1 - x, y), (x, 1 - y), (1 - x, 1 - y))
    places = []
    start = 0
    for columns in chunks:
        for px, py in owners:
            places.append(
                pl.ds(pl.multiple_of((py * 2 + px) * (width // 4) + start, 128), columns)
            )
        start += columns
    copies = []
    step = 16
    for i, top in enumerate(range(0, rows, step)):
        block = pl.ds(top, step)
        squares = jnp.zeros((step, 128), jnp.float32)
        for piece in pieces:
            for at in range(0, piece.shape[1], 128):
                value = piece[block, pl.ds(at, 128)].astype(jnp.float32)
                squares = squares + value * value
        scale = lax.rsqrt(jnp.sum(squares, axis=-1, keepdims=True) / width + norm_eps)
        for piece, at in zip(pieces, places):
            normed = piece[block, :].astype(jnp.float32) * scale * gain_ref[:, at]
            out_ref[block, at] = (hidden_ref[block, at].astype(jnp.float32) + normed).astype(
                jnp.bfloat16
            )
        copies.append(pltpu.make_async_copy(out_ref.at[block], out_hbm.at[block], sems.at[i]))
        copies[-1].start()
    for copy in copies:
        copy.wait()


def shards(ring, chunks, hidden_rows, query_proj, key_proj, value_proj, order_pos, post_gain, out_weight):
    n = len(ring)
    tokens = query_proj.shape[1]
    width = hidden_rows.shape[2]
    swap = [(0, 1), (1, 0)]
    along = [(ring[i], ring[(i + 1) % n]) for i in range(n)]

    def over(value, axis):
        if axis == "diag":
            return lax.ppermute(value, ("ctx", "x"), [(i, 3 - i) for i in range(4)])
        return lax.ppermute(value, axis, along if axis == "z" else swap)

    rows, block = out_weight.shape
    quarter = block // 2

    def call(body, outs, ins, name, scratch=(), label=None):
        return pl.pallas_call(
            body,
            out_shape=outs,
            in_specs=[VMEM] * ins,
            out_specs=[VMEM] * len(outs),
            scratch_shapes=scratch,
            compiler_params=params(),
            cost_estimate=pl.CostEstimate(
                flops=int(COSTS.get(label or name, 0) * PER_CYCLE) + 1, bytes_accessed=0, transcendentals=0
            ),
            name=name,
        )

    moves, kernels = {}, {}
    kernels["cut"] = (call(cut, [bf16(rows, quarter)] * 2, 1, "cut"), ("w",), ("a0", "awayo"))
    kernels["stage"] = (
        call(
            stage,
            [bf16(tokens, a.shape[2]) for a in (query_proj, key_proj, value_proj)]
            + [jax.ShapeDtypeStruct(order_pos.shape, jnp.int32)],
            4,
            "stage",
        ),
        ("qo", "Ko", "Vo", "poso"),
        ("q", "Kq", "Vq", "posq"),
    )
    wide = bf16(tokens, HQ * DH // ACTS)
    halves = "12"[:ACTS]
    for k, axis in (("K", "ctx"), ("V", "ctx"), ("pos", "ctx"), ("B0", "x")):
        moves[k] = ({"B0": "awayo"}.get(k, k + "o"), axis)
    kernels["att"] = (
        call(attend, [wide] * ACTS, 7, "attend", label="att"),
        ("q", "Kq", "K", "Vq", "V", "posq", "pos"),
        tuple("h" + i for i in halves),
    )
    for i in halves:
        moves["x" + i] = ("h" + i, "x")
        moves["y" + i] = ("h" + i, "ctx")
    if ACTS == 2:
        moves["d1"], moves["d2"] = ("y1", "x"), ("x2", "ctx")
        acts = ("h1", "h2", "x1", "x2", "y1", "y2", "d1", "d2")
        sizes = (2, 2, 2, 2)
    else:
        half = bf16(tokens, HQ * DH // 2)
        kernels["hy"] = (call(functools.partial(part, 0), [half], 1, "halves", label="hy"), ("y1",), ("y1l",))
        kernels["hx"] = (call(functools.partial(part, 1), [half], 1, "halves", label="hx"), ("x1",), ("x1r",))
        moves["d1"], moves["d2"] = ("y1l", "x"), ("x1r", "ctx")
        acts, sizes = ("h1", "x1", "y1", "d1", "d2"), (1, 1, 1, 2)
    for chain, whole in WHOLE_STEPS.items():
        for i in range(1, whole + 1):
            moves[chain + str(i)] = (chain + str(i - 1), "z")
        if whole < n - 1:
            last = chain + str(whole)
            kernels["split" + chain] = (
                call(split, [bf16(rows, c) for c in chunks], 1, "split", label="split" + chain),
                (last,),
                tuple("%s_%d" % (last, c) for c in range(len(chunks))),
            )
    def spot(name):
        return name[0], int(name[1:])

    sure = [spot(name) for names in PACKS for name in names]
    late = [(chain, i) for chain in WHOLE_STEPS for i in range(n) if (chain, i) not in sure]
    order, bufs = [], []
    for k, names in enumerate(PACKS):
        kernels["pk%d" % k] = (
            call(stack, [bf16(len(names) * rows, quarter)], len(names), "stack", label="pk%d" % k),
            tuple(names),
            ("k%d" % k,),
        )
        moves["ck%d" % k] = ("k%d" % k, "core")
        bufs += ["k%d" % k, "ck%d" % k]
        for same in (True, False):
            order += [(spot(name)[1], name[0] == "a", same) for name in names]
    done = len(order)
    order += [(i, chain == "a", same) for chain, i in late for same in (True, False)]
    three = (*acts[: 3 * ACTS],)
    kernels["early"] = (
        call(
            functools.partial(early, ring, (ACTS,) * 3, order[:done]),
            [
                jax.ShapeDtypeStruct((3 * tokens, quarter), jnp.float32),
                bf16(3 * tokens, HQ * DH),
                bf16(done * DH, quarter),
            ],
            len(three) + len(bufs),
            "early",
        ),
        (*three, *bufs),
        ("acc", "aall", "wall"),
    )
    for c, columns in enumerate(chunks):
        j = str(c)
        bufs = []
        for chain, i in late:
            name = "%s%d" % (chain, i) if i <= WHOLE_STEPS[chain] else "%s%d_%d" % (chain, i, c)
            if i > WHOLE_STEPS[chain]:
                moves[name] = ("%s%d_%d" % (chain, i - 1, c), "z")
            moves["c" + name] = (name, "core")
            bufs += [name, "c" + name]
        operands = ("acc", "aall", "wall", *acts[3 * ACTS :], *bufs)
        results = tuple("p" + k + j for k in "oxyd")
        kernels["proj" + j] = (
            call(
                functools.partial(project, ring, sum(chunks[:c]), (2,), order),
                [bf16(tokens, columns)] * 4,
                len(operands),
                "project",
                [pltpu.VMEM((tokens, HQ * DH), jnp.bfloat16)],
                label="proj" + j,
            ),
            operands,
            results,
        )
        for k, axis in zip("xyd", ("x", "ctx", "diag")):
            moves["r" + k + j] = ("p" + k + j, axis)

    held = dict(
        w=out_weight, qo=query_proj[0], Ko=key_proj[0], Vo=value_proj[0], poso=order_pos
    )

    def after(value, deps):
        for dep in deps:
            token, held[dep] = lax.optimization_barrier((lax.create_token(), held[dep]))
            token, value = lax.optimization_barrier((token, value))
        return value

    pending = list(kernels) + list(moves)
    while pending:
        for name in pending:
            sources, results = (moves[name][:1], (name,)) if name in moves else kernels[name][1:]
            deps = [d for d in TIES.get(name, ())]
            if all(k in held for k in (*sources, *deps)):
                break
        pending.remove(name)
        first = after(held[sources[0]], deps)
        if name in moves:
            held[name] = over(first, moves[name][1])
        else:
            out = kernels[name][0](first, *(held[k] for k in sources[1:]))
            held.update(zip(results, out))

    pieces = [held[("po" if k == "o" else "r" + k) + str(c)] for c in range(len(chunks)) for k in "oxyd"]

    out = pl.pallas_call(
        functools.partial(finish, chunks),
        out_shape=bf16(tokens, width),
        in_specs=[VMEM] * (2 + len(pieces)),
        out_specs=HBM,
        scratch_shapes=[
            pltpu.VMEM((tokens, width), jnp.bfloat16),
            pltpu.SemaphoreType.DMA((tokens // 16,)),
        ],
        compiler_params=params(),
        cost_estimate=pl.CostEstimate(flops=1, bytes_accessed=0, transcendentals=0),
        name="finish",
    )(hidden_rows[0], post_gain.reshape(1, width), *pieces)
    return out[None]


def plain_shards(hidden_rows, query_proj, key_proj, value_proj, order_pos, post_gain, out_weight):
    tokens = query_proj.shape[1]
    groups = HQ // HK
    positions = lax.all_gather(order_pos, "ctx", axis=1, tiled=True)[0]
    weight_block = lax.all_gather(out_weight, "fsdp", axis=0, tiled=True)
    query = query_proj[0].reshape(tokens, HK, groups, DH)
    keys = lax.all_gather(key_proj, "ctx", axis=1, tiled=True)[0].reshape(-1, HK, DH)
    values = lax.all_gather(value_proj, "ctx", axis=1, tiled=True)[0].reshape(-1, HK, DH)
    scores = jnp.einsum("thgd,nhd->hgtn", query, keys, preferred_element_type=jnp.float32)
    capped = soft_cap * jnp.tanh(scores * score_scale / soft_cap)
    visible = positions[None, :] <= order_pos[0][:, None]
    weights = jnp.where(visible, jnp.exp(capped), 0.0)
    numerator = jnp.einsum(
        "hgtn,nhd->thgd", weights.astype(jnp.bfloat16), values, preferred_element_type=jnp.float32
    )
    denominator = jnp.transpose(jnp.sum(weights, axis=-1), (2, 0, 1))
    attended = (numerator / denominator[..., None]).astype(jnp.bfloat16).reshape(1, tokens, HQ * DH)
    projected = jnp.dot(
        lax.all_gather(attended, "ctx", axis=1, tiled=True)[0],
        weight_block,
        preferred_element_type=jnp.float32,
    )
    token_rows = lax.all_to_all(
        projected.astype(jnp.bfloat16), "ctx", split_axis=0, concat_axis=1, tiled=True
    ).astype(jnp.float32)
    mean = jnp.mean(token_rows * token_rows, axis=-1, keepdims=True)
    normed = token_rows * lax.rsqrt(mean + norm_eps) * post_gain
    return (hidden_rows[0].astype(jnp.float32) + normed).astype(jnp.bfloat16)[None]


def solution(mesh):
    ctx, fsdp = mesh.shape["ctx"], mesh.shape["fsdp"]
    rows = "fsdp"
    body = plain_shards
    if ctx == 2 and fsdp % 4 == 0 and fsdp == HQ:
        mesh = Mesh(np.asarray(mesh.devices).reshape(ctx, fsdp // 4, 2, 2), ("ctx", "z", "x", "core"))
        rows = ("z", "x", "core")
        body = functools.partial(shards, ring_of(fsdp // 4), CHUNKS)
    placed = (
        P(rows, "ctx", None),
        P(rows, "ctx", None),
        P(rows, "ctx", None),
        P(rows, "ctx", None),
        P(rows, "ctx"),
        P(),
        P(rows, "ctx"),
    )
    return jax.shard_map(
        body, mesh=mesh, in_specs=placed, out_specs=P(rows, "ctx", None), check_vma=False
    )
```
